128 devices in a mesh: expert: 32 (over z, x, core), dp: 4 (over y).
Axes of the slice: x: 4, y: 4, z: 4, core: 2. Of those that a mesh axis runs over, the one named last changes fastest.
Arguments:
- tokens: bfloat16 [24576, 1024], P(('expert', 'dp')), may hold values from -96 to 96
- out_grad: bfloat16 [24576, 1024], P(('expert', 'dp')), may hold values from -6 to 6
- routes: int32 [24576, 2], P(('expert', 'dp')), may hold values from 0 to 31, all different within a row
- router_weight: float32 [1024, 32], replicated, may hold values from -0.5 to 0.5
- gate_weight: bfloat16 [32, 2816, 1024], P('expert'), may hold values from -0.1875 to 0.1875
- up_weight: bfloat16 [32, 2816, 1024], P('expert'), may hold values from -0.1875 to 0.1875
- down_weight: bfloat16 [32, 2816, 1024], P('expert'), may hold values from -0.109375 to 0.109375
Outputs:
- in_grad: bfloat16 [24576, 1024], P(('expert', 'dp'))
- grad_experts: bfloat16 [32, 2816, 3, 1024], P('expert', 'dp')
- grad_router: float32 [1024, 32], replicated
The draws below stay inside these ranges and needn't reach their ends.
Inputs may be any that keep to these rules, and one draw needn't show every extreme that they name: `routes`: each row names two different experts, and every expert is named by some row.
All inputs are finite; a program needn't handle non-finite values.
Results may differ from the reference program's by a relative error of at most 0.015.
Values may be sent and summed in bfloat16 or wider, within the bound.
No kernel may reach another device: no remote copies, remote signals or barrier semaphores. Data moves between devices by JAX's collectives and lax.ppermute only.
A program may use at most 192 MiB of HBM per device.

```python
import math
from functools import partial
import jax
import jax.numpy as jnp
from jax import lax

D = 1024
FF = 2816
TOP = 2
TOK_DEV = 192
EXPERTS = 32
CAP = 15
TOKENS = 24576
N_EXPERT = 32
N_DP = 4


def router_base(key):
    columns = jax.random.normal(key, (D, EXPERTS), jnp.float32) * (2.0 / math.sqrt(D))
    return jnp.clip(columns, -0.5, 0.5)


def draw_router_weight(key, part):
    return router_base(key)


def draw_tokens(key, part):
    key = jax.random.fold_in(key, 7)
    values = jnp.clip(jax.random.normal(key, (TOKENS, D), jnp.float32), -6.0, 6.0)
    return values.astype(jnp.bfloat16)


def block_scale(own_key, extent, cuts, low, high):
    loudness = 1.0
    for dim, shards_of in cuts:
        heights = jax.random.uniform(jax.random.fold_in(jax.random.fold_in(own_key, 6), dim), (shards_of,), jnp.float32, low / len(cuts), high / len(cuts))
        loudness = loudness * jnp.repeat(jnp.exp(heights), extent[dim] // shards_of).reshape((-1,) + (1,) * (len(extent) - 1 - dim))
    return loudness


def picks_of(own_key, rows, number_of, top, lift):
    ranking = jax.random.permutation(jax.random.fold_in(own_key, 1), number_of)
    favour = ranking
    for power in range(3):
        favour = favour * favour // number_of
    favour = favour * lift // number_of
    chance = jax.random.randint(jax.random.fold_in(own_key, 2), (rows, number_of), 0, 4096) + favour
    fixed_rows = jax.random.permutation(jax.random.fold_in(own_key, 3), rows)[jnp.arange(number_of) % rows]
    chance = jnp.where(jnp.arange(rows)[:, None] == fixed_rows[None, :], 1 << 14, chance)
    score = chance * number_of + jnp.arange(number_of)
    return lax.top_k(score.astype(jnp.int32), top)[1].astype(jnp.int32)


def gaussian(stream_key, extent, width, reach, pieces=(), kind=jnp.bfloat16):
    result = width * jax.random.normal(stream_key, extent, jnp.float32)
    if pieces:
        result = result * block_scale(stream_key, extent, pieces, -0.22, 0.18)
    return jnp.clip(result, -reach, reach).astype(kind)


def setup_inputs(seed: int = 0) -> dict:
    keys = jax.random.split(jax.random.key(seed), 8)
    return {
        "tokens": draw_tokens(jax.random.fold_in(keys[7], 71), 0),
        "out_grad": gaussian(keys[1], (TOKENS, D), 1.0, 6.0, ((0, 128),)),
        "routes": picks_of(keys[2], TOKENS, EXPERTS, TOP, 1024),
        "router_weight": draw_router_weight(jax.random.fold_in(keys[7], 71), 0),
        "gate_weight": gaussian(keys[4], (EXPERTS, FF, D), D ** -0.5, 0.1875, ((0, 32),)),
        "up_weight": gaussian(keys[5], (EXPERTS, FF, D), D ** -0.5, 0.1875, ((0, 32),)),
        "down_weight": gaussian(keys[6], (EXPERTS, FF, D), FF ** -0.5, 0.109375, ((0, 32),)),
    }


SQRT_TWO_OVER_PI = 0.7978845608
CUBIC_COEF = 0.044715


def gelu_parts(values):
    tanh_value = jnp.tanh(SQRT_TWO_OVER_PI * (values + CUBIC_COEF * values * values * values))
    gelu_value = 0.5 * values * (1.0 + tanh_value)
    gelu_slope = 0.5 * (1.0 + tanh_value) + 0.5 * values * (1.0 - tanh_value * tanh_value) * SQRT_TWO_OVER_PI * (1.0 + 3.0 * CUBIC_COEF * values * values)
    return gelu_value, gelu_slope


def route_masks(routes, experts, capacity):
    count_tok = routes.shape[0]
    expert_ids = jnp.arange(experts, dtype=jnp.int32)
    onehot = (routes.T[:, :, None] == expert_ids[None, None, :]).astype(jnp.int32)
    flat_hits = onehot.reshape(2 * count_tok, experts)
    position = jnp.sum(jnp.cumsum(flat_hits, 0, dtype=jnp.int32) * flat_hits, 1, dtype=jnp.int32) - 1
    slot_index = routes.T.reshape(-1) * capacity + position
    slot_index = jnp.where(position < capacity, slot_index, -1).reshape(2, count_tok)
    slot_ids = jnp.arange(experts * capacity, dtype=jnp.int32)
    slot_masks = (slot_ids[None, :, None] == slot_index[:, None, :]).astype(jnp.bfloat16)
    return onehot.astype(jnp.float32), slot_masks


def source_side(tokens, out_grad, routes, router_weight, capacity):
    logits = jnp.dot(tokens.astype(jnp.float32), router_weight, precision=lax.Precision.HIGHEST)
    router_probs = jax.nn.softmax(logits, -1)
    onehot, slot_masks = route_masks(routes, router_weight.shape[1], capacity)
    gate_values = jnp.sum(onehot * router_probs[None], -1)
    scaled = (gate_values[:, :, None] * out_grad.astype(jnp.float32)[None]).astype(jnp.bfloat16)
    either_mask = slot_masks[0] + slot_masks[1]
    sent_rows = jnp.dot(either_mask, tokens, preferred_element_type=jnp.float32).astype(jnp.bfloat16)
    sent_grads = (jnp.dot(slot_masks[0], scaled[0], preferred_element_type=jnp.float32) + jnp.dot(slot_masks[1], scaled[1], preferred_element_type=jnp.float32)).astype(jnp.bfloat16)
    return router_probs, onehot, slot_masks, sent_rows, sent_grads


def contract_rows(left, right):
    return lax.dot_general(left, right, (((0,), (0,)), ((), ())), preferred_element_type=jnp.float32)


def expert_pass(rows_x, rows_dy, w_gate, w_up, w_down):
    feature_dims = (((1,), (1,)), ((), ()))
    gate_pre = lax.dot_general(rows_x, w_gate, feature_dims, preferred_element_type=jnp.float32)
    up_pre = lax.dot_general(rows_x, w_up, feature_dims, preferred_element_type=jnp.float32)
    gelu_value, gelu_slope = gelu_parts(gate_pre)
    activated = (gelu_value * up_pre).astype(jnp.bfloat16)
    expert_outs = jnp.dot(activated, w_down, preferred_element_type=jnp.float32)
    hidden_grad = lax.dot_general(rows_dy, w_down, feature_dims, preferred_element_type=jnp.float32)
    pre_gate_grad = (hidden_grad * up_pre * gelu_slope).astype(jnp.bfloat16)
    pre_up_grad = (hidden_grad * gelu_value).astype(jnp.bfloat16)
    row_grads = jnp.dot(pre_gate_grad, w_gate, preferred_element_type=jnp.float32) + jnp.dot(pre_up_grad, w_up, preferred_element_type=jnp.float32)
    return row_grads, expert_outs, activated, pre_gate_grad, pre_up_grad


def weight_terms(rows_x, rows_dy, activated, pre_gate_grad, pre_up_grad):
    return jnp.stack([contract_rows(pre_gate_grad, rows_x), contract_rows(pre_up_grad, rows_x), contract_rows(activated, rows_dy)], 1)


def source_finish(tokens, out_grad, router_weight, router_probs, onehot, slot_masks, back_rows, back_outs):
    either_mask = slot_masks[0] + slot_masks[1]
    expert_part = contract_rows(either_mask, back_rows)
    first_outs = contract_rows(slot_masks[0], back_outs)
    second_outs = contract_rows(slot_masks[1], back_outs)
    grad_float = out_grad.astype(jnp.float32)
    gate_grads = jnp.stack([jnp.sum(grad_float * first_outs, -1), jnp.sum(grad_float * second_outs, -1)])
    prob_grads = jnp.sum(onehot * gate_grads[:, :, None], 0)
    logit_grads = router_probs * (prob_grads - jnp.sum(router_probs * prob_grads, -1, keepdims=True))
    in_grad = (expert_part + jnp.dot(logit_grads, router_weight.T, precision=lax.Precision.HIGHEST)).astype(jnp.bfloat16)
    router_term = jnp.dot(tokens.astype(jnp.float32).T, logit_grads, precision=lax.Precision.HIGHEST)
    return in_grad, router_term


def reference(tokens, out_grad, routes, router_weight, gate_weight, up_weight, down_weight):
    blocks = N_EXPERT * N_DP
    token_blocks = tokens.reshape(blocks, TOK_DEV, D)
    grad_blocks = out_grad.reshape(blocks, TOK_DEV, D)
    route_blocks = routes.reshape(blocks, TOK_DEV, TOP)
    prepare = jax.vmap(partial(source_side, capacity=CAP), in_axes=(0, 0, 0, None))
    router_probs, onehot, slot_masks, sent_rows, sent_grads = prepare(token_blocks, grad_blocks, route_blocks, router_weight)
    expert_rows = sent_rows.reshape(blocks, EXPERTS, CAP, D).transpose(1, 0, 2, 3).reshape(EXPERTS, blocks * CAP, D)
    expert_grads = sent_grads.reshape(blocks, EXPERTS, CAP, D).transpose(1, 0, 2, 3).reshape(EXPERTS, blocks * CAP, D)

    def one_expert(items):
        rows_x, rows_dy, w_gate, w_up, w_down = items
        row_grads, expert_outs, activated, pre_gate_grad, pre_up_grad = expert_pass(rows_x, rows_dy, w_gate, w_up, w_down)
        grads = weight_terms(rows_x, rows_dy, activated, pre_gate_grad, pre_up_grad).astype(jnp.bfloat16)
        return row_grads.astype(jnp.bfloat16), expert_outs.astype(jnp.bfloat16), grads

    row_grads, expert_outs, grad_experts = lax.map(one_expert, (expert_rows, expert_grads, gate_weight, up_weight, down_weight))
    back_rows = row_grads.reshape(EXPERTS, blocks, CAP, D).transpose(1, 0, 2, 3).reshape(blocks, EXPERTS * CAP, D)
    back_outs = expert_outs.reshape(EXPERTS, blocks, CAP, D).transpose(1, 0, 2, 3).reshape(blocks, EXPERTS * CAP, D)
    finish = jax.vmap(source_finish, in_axes=(0, 0, None, 0, 0, 0, 0, 0))
    in_grad, router_terms = finish(token_blocks, grad_blocks, router_weight, router_probs, onehot, slot_masks, back_rows, back_outs)
    return in_grad.reshape(TOKENS, D), grad_experts, jnp.sum(router_terms, 0)
```

```python
import functools
import jax
import jax.numpy as jnp
from jax import lax
from jax.experimental import pallas as pl
from jax.experimental.pallas import tpu as pltpu
from jax.sharding import PartitionSpec as P

SQRT_TWO_OVER_PI = 0.7978845608
CUBIC_COEF = 0.044715
STRIDE = 16
F32 = jnp.float32
BF16 = jnp.bfloat16
VMEM_LIMIT = 60 * 1024 * 1024

FEATURE_DIMS = (((1,), (1,)), ((), ()))
ROW_DIMS = (((0,), (0,)), ((), ()))


def dot(left, right, dims=(((1,), (0,)), ((), ()))):
    return lax.dot_general(left, right, dims, preferred_element_type=F32)


def gelu_parts(values):
    square = values * values
    tanh_value = jnp.tanh(values * (SQRT_TWO_OVER_PI + (SQRT_TWO_OVER_PI * CUBIC_COEF) * square))
    half = 0.5 + 0.5 * tanh_value
    slope = half + (half * (1.0 - tanh_value)) * values * (
        SQRT_TWO_OVER_PI + (3.0 * CUBIC_COEF * SQRT_TWO_OVER_PI) * square
    )
    return (values * half, slope)


def split_three(values):
    high = values.astype(BF16)
    rest = values - high.astype(F32)
    mid = rest.astype(BF16)
    low = (rest - mid.astype(F32)).astype(BF16)
    return (high, mid, low)


def softmax(logits, axis):
    shifted = jnp.exp(logits - jnp.max(logits, axis, keepdims=True))
    return shifted / jnp.sum(shifted, axis, keepdims=True)


def slot_rows(routes, experts, capacity):
    count_tok = routes.shape[1]
    expert_ids = lax.broadcasted_iota(jnp.int32, (experts, count_tok), 0)
    first = expert_ids == routes[0:1, :]
    second = expert_ids == routes[1:2, :]
    earlier = (
        lax.broadcasted_iota(jnp.int32, (count_tok, count_tok), 0)
        < lax.broadcasted_iota(jnp.int32, (count_tok, count_tok), 1)
    ).astype(BF16)
    first_hits = first.astype(F32)
    second_hits = second.astype(F32)
    first_before = dot(first_hits.astype(BF16), earlier)
    second_before = dot(second_hits.astype(BF16), earlier) + jnp.sum(first_hits, 1, keepdims=True)
    first_pos = jnp.sum(first_hits * first_before, 0, keepdims=True)
    second_pos = jnp.sum(second_hits * second_before, 0, keepdims=True)
    slots = []
    for pos, route in ((first_pos, routes[0:1, :]), (second_pos, routes[1:2, :])):
        pos = pos.astype(jnp.int32)
        slots.append(jnp.where(pos < capacity, route * STRIDE + pos, -1))
    return slots


def slot_mask(slots, experts):
    count_tok = slots[0].shape[1]
    slot_ids = lax.broadcasted_iota(jnp.int32, (experts * STRIDE, count_tok), 0)
    return ((slot_ids == slots[0]) | (slot_ids == slots[1])).astype(F32).astype(BF16)


def dispatch_kernel(experts, capacity, tokens, out_grad, routes, sent_rows, sent_grads):
    mask = slot_mask(slot_rows(routes[...], experts, capacity), experts)
    sent_rows[...] = dot(mask, tokens[...]).astype(BF16)
    sent_grads[...] = dot(mask, out_grad[...]).astype(BF16)


def combine_kernel(experts, capacity, routes, back, in_grad):
    mask = slot_mask(slot_rows(routes[...], experts, capacity), experts)
    in_grad[...] = dot(mask, back[...], ROW_DIMS).astype(BF16)


def expert_kernel(
    expert, rows_x, rows_g, router, w_gate, w_up, w_down, row_grads, router_term, total, gates, hits
):
    step = pl.program_id(0)
    last = pl.num_programs(0) - 1

    @pl.when(step == 0)
    def _():
        high, mid, low = split_three(router[...])
        stacked = jnp.concatenate([high, mid, low], 0)
        count = router.shape[0]
        parts = dot(rows_x[...], stacked, FEATURE_DIMS)
        logits = parts[:, :count] + parts[:, count : 2 * count] + parts[:, 2 * count :]
        gates[...] = softmax(logits, 1)
        total[...] = jnp.zeros_like(total)
        hits[...] = jnp.zeros_like(hits)

    probs = gates[...]
    mine = lax.broadcasted_iota(jnp.int32, probs.shape, 1) == expert[0]
    gate = jnp.sum(jnp.where(mine, probs, 0.0), 1, keepdims=True)
    gate_pre = dot(rows_x[...], w_gate[...], FEATURE_DIMS)
    up_pre = dot(rows_x[...], w_up[...], FEATURE_DIMS)
    raw_grad = dot(rows_g[...], w_down[...], FEATURE_DIMS)
    gelu_value, gelu_slope = gelu_parts(gate_pre)
    hits[...] += jnp.sum(gelu_value * up_pre * raw_grad, 1, keepdims=True)
    hidden_grad = raw_grad * gate
    pre_gate_grad = (hidden_grad * up_pre * gelu_slope).astype(BF16)
    pre_up_grad = (hidden_grad * gelu_value).astype(BF16)
    total[...] += dot(pre_gate_grad, w_gate[...]) + dot(pre_up_grad, w_up[...])

    @pl.when(step == last)
    def _():
        high, mid, low = split_three(router[...])
        logit_grads = hits[...] * gate * (mine.astype(F32) - probs)
        logit_high = logit_grads.astype(BF16)
        logit_low = (logit_grads - logit_high.astype(F32)).astype(BF16)
        router_part = dot(logit_high, high) + dot(logit_high, mid) + dot(logit_low, high)
        row_grads[...] = (total[...] + router_part).astype(BF16)
        router_term[...] = dot(logit_high, rows_x[...], ROW_DIMS) + dot(
            logit_low, rows_x[...], ROW_DIMS
        )


def weight_kernel(pieces, first, last, *refs):
    place, router, w_gate, w_up, w_down = refs[:5]
    rows = refs[5 : 5 + 2 * pieces]
    rest = refs[5 + 2 * pieces :]
    if first:
        (out,) = rest
    else:
        before, out = rest
    high, mid, low = split_three(router[...])
    stacked = jnp.concatenate([high, mid, low], 0)
    count = router.shape[0]
    sums = [None, None, None] if first else [before[k] for k in range(3)]
    for piece in range(pieces):
        rows_x = rows[2 * piece][...]
        rows_g = rows[2 * piece + 1][...]
        parts = dot(stacked, rows_x, FEATURE_DIMS)
        probs = softmax(parts[:count] + parts[count : 2 * count] + parts[2 * count :], 0)
        mine = lax.broadcasted_iota(jnp.int32, probs.shape, 0) == place[0]
        gate = jnp.sum(jnp.where(mine, probs, 0.0), 0, keepdims=True)
        gate_pre = dot(w_gate[...], rows_x, FEATURE_DIMS)
        up_pre = dot(w_up[...], rows_x, FEATURE_DIMS)
        hidden_grad = dot(w_down[...], rows_g, FEATURE_DIMS) * gate
        gelu_value, gelu_slope = gelu_parts(gate_pre)
        activated = (gelu_value * up_pre * gate).astype(BF16)
        pre_gate_grad = (hidden_grad * up_pre * gelu_slope).astype(BF16)
        pre_up_grad = (hidden_grad * gelu_value).astype(BF16)
        terms = (dot(pre_gate_grad, rows_x), dot(pre_up_grad, rows_x), dot(activated, rows_g))
        sums = [t if s is None else s + t for s, t in zip(sums, terms)]
    for k in range(3):
        out[k] = sums[k].astype(out.dtype)


def run_dispatch(tokens, out_grad, routes, experts, capacity):
    shape = jax.ShapeDtypeStruct((experts * STRIDE, tokens.shape[1]), BF16)
    return pl.pallas_call(
        functools.partial(dispatch_kernel, experts, capacity),
        out_shape=(shape, shape),
        compiler_params=pltpu.CompilerParams(vmem_limit_bytes=VMEM_LIMIT),
        name="dispatch",
    )(tokens, out_grad, routes)


def run_combine(routes, back, experts, capacity):
    return pl.pallas_call(
        functools.partial(combine_kernel, experts, capacity),
        out_shape=jax.ShapeDtypeStruct((routes.shape[1], back.shape[1]), BF16),
        compiler_params=pltpu.CompilerParams(vmem_limit_bytes=VMEM_LIMIT),
        name="combine",
    )(routes, back)


def run_expert(expert, rows_x, rows_g, router, w_gate, w_up, w_down, tile=256):
    rows, features = rows_x.shape
    hidden = w_gate.shape[1]
    experts = router.shape[0]
    whole = lambda shape: pl.BlockSpec(shape, lambda i: (0, 0))
    weight = pl.BlockSpec((None, tile, features), lambda i: (0, i, 0))
    return pl.pallas_call(
        expert_kernel,
        grid=(hidden // tile,),
        in_specs=[
            pl.BlockSpec(memory_space=pltpu.SMEM),
            whole((rows, features)),
            whole((rows, features)),
            whole((experts, features)),
            weight,
            weight,
            weight,
        ],
        out_specs=(whole((rows, features)), whole((experts, features))),
        out_shape=(
            jax.ShapeDtypeStruct((rows, features), BF16),
            jax.ShapeDtypeStruct((experts, features), F32),
        ),
        scratch_shapes=[
            pltpu.VMEM((rows, features), F32),
            pltpu.VMEM((rows, experts), F32),
            pltpu.VMEM((rows, 1), F32),
        ],
        compiler_params=pltpu.CompilerParams(vmem_limit_bytes=VMEM_LIMIT),
        cost_estimate=pl.CostEstimate(
            flops=10 * rows * hidden * features,
            bytes_accessed=6 * hidden * features + 6 * rows * features,
            transcendentals=rows * hidden,
        ),
        name="expert_pass",
    )(expert, rows_x, rows_g, router, w_gate, w_up, w_down)


def run_weight(place, router, weights, pieces, before, out_dtype, slices, tile):
    features = router.shape[1]
    hidden = weights[0].shape[1] // slices
    steps = hidden // tile
    whole = lambda shape: pl.BlockSpec(shape, lambda i, p: (0, 0))
    weight = pl.BlockSpec((None, tile, features), lambda i, p: (0, p[1] * steps + i, 0))
    grads = pl.BlockSpec((3, tile, features), lambda i, p: (0, i, 0))
    rows = [r for piece in pieces for r in piece]
    count = sum(x.shape[0] for x, _ in pieces)
    return pl.pallas_call(
        functools.partial(weight_kernel, len(pieces), before is None, True),
        grid_spec=pltpu.PrefetchScalarGridSpec(
            num_scalar_prefetch=1,
            grid=(steps,),
            in_specs=[whole(router.shape), weight, weight, weight]
            + [whole(r.shape) for r in rows]
            + ([] if before is None else [grads]),
            out_specs=grads,
        ),
        out_shape=jax.ShapeDtypeStruct((3, hidden, features), out_dtype),
        compiler_params=pltpu.CompilerParams(vmem_limit_bytes=VMEM_LIMIT),
        cost_estimate=pl.CostEstimate(
            flops=12 * count * hidden * features,
            bytes_accessed=6 * hidden * features + 4 * count * features + 12 * hidden * features,
            transcendentals=count * hidden,
        ),
        name="weight_grads",
    )(place, router, *weights, *rows, *([] if before is None else [before]))


def exchange(rows, axis, stride):
    return lax.all_to_all(rows, axis, split_axis=0, concat_axis=0, tiled=True)


def shift(value, axis, step):
    size = lax.axis_size(axis)
    return lax.ppermute(value, axis, [(i, (i + step) % size) for i in range(size)])


def sum_over(value, axis):
    size = lax.axis_size(axis)
    bit = 1
    while bit < size:
        value = value + lax.ppermute(value, axis, [(i, i ^ bit) for i in range(size)])
        bit *= 2
    return value


def shards(tokens, out_grad, routes, router_weight, gate_weight, up_weight, down_weight):
    count_tok, features = tokens.shape
    experts = router_weight.shape[1]
    capacity = 5 * count_tok * 2 // (4 * experts)
    routes_t = routes.T
    router = router_weight.T
    weights = (gate_weight, up_weight, down_weight)
    expert = lax.axis_index("expert").astype(jnp.int32)
    group = lax.axis_index("dp").astype(jnp.int32)

    sent_rows, sent_grads = run_dispatch(tokens, out_grad, routes_t, experts, capacity)

    def arrive(sent):
        got = lax.all_to_all(
            sent.reshape(experts, STRIDE, features),
            "expert",
            split_axis=0,
            concat_axis=0,
            tiled=True,
        )
        return got[:, :capacity].reshape(experts * capacity, features)

    rows_x = arrive(sent_rows)
    rows_g = arrive(sent_grads)
    half = rows_x.shape[0] // 2
    left_x, right_x = shift(rows_x, "dp", 1), shift(rows_x, "dp", -1)
    left_g, right_g = shift(rows_g, "dp", 1), shift(rows_g, "dp", -1)
    far_x = (shift(left_x[:half], "dp", 1), shift(right_x[half:], "dp", -1))
    far_g = (shift(left_g[:half], "dp", 1), shift(right_g[half:], "dp", -1))

    row_grads, router_term = run_expert(
        jnp.stack([expert]), rows_x, rows_g, router, *weights
    )
    back = jnp.pad(
        row_grads.reshape(experts, capacity, features), ((0, 0), (0, STRIDE - capacity), (0, 0))
    )
    back = lax.all_to_all(back, "expert", split_axis=0, concat_axis=0, tiled=True)
    in_grad = run_combine(routes_t, back.reshape(-1, features), experts, capacity)
    grad_router = sum_over(sum_over(router_term, "expert"), "dp").T

    place = jnp.stack([expert, group])
    slices = lax.axis_size("dp")
    near = run_weight(
        place,
        router,
        weights,
        [(rows_x, rows_g), (left_x, left_g), (right_x, right_g)],
        None,
        F32,
        slices,
        352,
    )
    grads = run_weight(
        place,
        router,
        weights,
        list(zip(far_x, far_g)),
        near,
        BF16,
        slices,
        352,
    )
    return (in_grad, jnp.transpose(grads, (1, 0, 2))[None], grad_router)


def solution(mesh):
    in_specs = (
        P(("expert", "dp"), None),
        P(("expert", "dp"), None),
        P(("expert", "dp"), None),
        P(),
        P("expert", None, None),
        P("expert", None, None),
        P("expert", None, None),
    )
    out_specs = (P(("expert", "dp"), None), P("expert", "dp", None, None), P())
    return jax.shard_map(shards, mesh=mesh, in_specs=in_specs, out_specs=out_specs, check_vma=False)
```

```python
import functools
import jax
import jax.numpy as jnp
from jax import lax
from jax.experimental import pallas as pl
from jax.experimental.pallas import tpu as pltpu
from jax.sharding import PartitionSpec as P

SQRT_TWO_OVER_PI = 0.7978845608
CUBIC_COEF = 0.044715
STRIDE = 16
F32 = jnp.float32
BF16 = jnp.bfloat16
VMEM_LIMIT = 60 * 1024 * 1024

FEATURE_DIMS = (((1,), (1,)), ((), ()))
ROW_DIMS = (((0,), (0,)), ((), ()))


def dot(left, right, dims=(((1,), (0,)), ((), ()))):
    return lax.dot_general(left, right, dims, preferred_element_type=F32)


def gelu_parts(values):
    square = values * values
    tanh_value = jnp.tanh(values * (SQRT_TWO_OVER_PI + (SQRT_TWO_OVER_PI * CUBIC_COEF) * square))
    half = 0.5 + 0.5 * tanh_value
    slope = half + (half * (1.0 - tanh_value)) * values * (
        SQRT_TWO_OVER_PI + (3.0 * CUBIC_COEF * SQRT_TWO_OVER_PI) * square
    )
    return (values * half, slope)


def split_three(values):
    high = values.astype(BF16)
    rest = values - high.astype(F32)
    mid = rest.astype(BF16)
    low = (rest - mid.astype(F32)).astype(BF16)
    return (high, mid, low)


def softmax(logits, axis):
    shifted = jnp.exp(logits - jnp.max(logits, axis, keepdims=True))
    return shifted / jnp.sum(shifted, axis, keepdims=True)


def slot_rows(routes, experts, capacity):
    count_tok = routes.shape[1]
    expert_ids = lax.broadcasted_iota(jnp.int32, (experts, count_tok), 0)
    first = expert_ids == routes[0:1, :]
    second = expert_ids == routes[1:2, :]
    earlier = (
        lax.broadcasted_iota(jnp.int32, (count_tok, count_tok), 0)
        < lax.broadcasted_iota(jnp.int32, (count_tok, count_tok), 1)
    ).astype(BF16)
    first_hits = first.astype(F32)
    second_hits = second.astype(F32)
    first_before = dot(first_hits.astype(BF16), earlier)
    second_before = dot(second_hits.astype(BF16), earlier) + jnp.sum(first_hits, 1, keepdims=True)
    first_pos = jnp.sum(first_hits * first_before, 0, keepdims=True)
    second_pos = jnp.sum(second_hits * second_before, 0, keepdims=True)
    slots = []
    for pos, route in ((first_pos, routes[0:1, :]), (second_pos, routes[1:2, :])):
        pos = pos.astype(jnp.int32)
        slots.append(jnp.where(pos < capacity, route * STRIDE + pos, -1))
    return slots


def slot_mask(slots, experts):
    count_tok = slots[0].shape[1]
    slot_ids = lax.broadcasted_iota(jnp.int32, (experts * STRIDE, count_tok), 0)
    return ((slot_ids == slots[0]) | (slot_ids == slots[1])).astype(F32).astype(BF16)


def dispatch_kernel(experts, capacity, tokens, out_grad, routes, sent):
    mask = slot_mask(slot_rows(routes[...], experts, capacity), experts)
    for k, source in enumerate((tokens, out_grad)):
        rows = dot(mask, source[...]).astype(BF16).reshape(experts, STRIDE, source.shape[1])
        sent[:, k * STRIDE : (k + 1) * STRIDE, :] = rows


def combine_kernel(experts, capacity, routes, back, spread, after, in_grad, grad_router):
    mask = slot_mask(slot_rows(routes[...], experts, capacity), experts)
    in_grad[...] = dot(mask, back[...], ROW_DIMS).astype(BF16)
    devices, chunks, lanes = spread.shape
    summed = jnp.sum(spread[...].reshape(experts, devices // experts, chunks, lanes), 1)
    for c in range(chunks):
        grad_router[:, c * lanes : (c + 1) * lanes] = summed[:, c, :]


def expert_kernel(tile, tiles, *refs):
    place, router = refs[:2]
    weights = refs[2:5]
    got = refs[5]
    (
        row_grads,
        w_gate,
        w_up,
        w_down,
        total,
        hits,
        even,
        odd,
        arrived,
    ) = refs[-9:]
    held = (w_gate, w_up, w_down)
    rows = hits.shape[0]
    count = router.shape[0]
    lanes = hits.shape[1]

    features = got.shape[3]

    def rows_x():
        return got[:, 0].reshape(rows, features)

    def rows_g():
        return got[:, 1].reshape(rows, features)

    def weight_copies(i):
        part = pl.ds(i * tile, tile)
        return [
            pltpu.make_async_copy(weights[k].at[0, part, :], held[k].at[part, :], arrived.at[k, i])
            for k in range(3)
        ]

    for i in range(tiles):
        for copy in weight_copies(i):
            copy.start()
    total[...] = jnp.zeros_like(total)
    hits[...] = jnp.zeros_like(hits)
    high, mid, low = split_three(router[...])
    parts = dot(rows_x(), jnp.concatenate([high, mid, low], 0), FEATURE_DIMS)
    probs = softmax(parts[:, :count] + parts[:, count : 2 * count] + parts[:, 2 * count :], 1)
    mine = lax.broadcasted_iota(jnp.int32, probs.shape, 1) == place[0]
    gate = jnp.sum(jnp.where(mine, probs, 0.0), 1, keepdims=True)
    gate_wide = jnp.broadcast_to(gate, (rows, tile))

    def wait(i):
        for copy in weight_copies(i):
            copy.wait()

    def part(i):
        return pl.ds(pl.multiple_of(i * tile, tile), tile)

    def before(i, slot):
        slot[0] = dot(rows_x(), w_gate[part(i), :], FEATURE_DIMS)
        slot[1] = dot(rows_x(), w_up[part(i), :], FEATURE_DIMS)
        slot[2] = dot(rows_g(), w_down[part(i), :], FEATURE_DIMS)

    def after(i, slot):
        gelu_value, gelu_slope = gelu_parts(slot[0])
        up_pre = slot[1]
        raw_grad = slot[2]
        hit = gelu_value * up_pre * raw_grad
        hits[...] += sum(hit[:, c : c + lanes] for c in range(0, tile, lanes))
        hidden_grad = raw_grad * gate_wide
        pre_gate_grad = (hidden_grad * up_pre * gelu_slope).astype(BF16)
        pre_up_grad = (hidden_grad * gelu_value).astype(BF16)
        total[...] += dot(pre_gate_grad, w_gate[part(i), :]) + dot(pre_up_grad, w_up[part(i), :])

    wait(0)
    before(0, even)

    def pair(j, carry):
        wait(2 * j + 1)
        wait(2 * j + 2)
        before(2 * j + 1, odd)
        after(2 * j, even)
        before(2 * j + 2, even)
        after(2 * j + 1, odd)
        return carry

    lax.fori_loop(0, (tiles - 1) // 2, pair, 0)
    if tiles % 2 == 0:
        wait(tiles - 1)
        before(tiles - 1, odd)
        after(tiles - 2, even)
        after(tiles - 1, odd)
    else:
        after(tiles - 1, even)

    logit_grads = jnp.sum(hits[...], 1, keepdims=True) * gate * (mine.astype(F32) - probs)
    logit_high = logit_grads.astype(BF16)
    logit_low = (logit_grads - logit_high.astype(F32)).astype(BF16)
    router_part = dot(logit_high, high) + dot(logit_high, mid) + dot(logit_low, high)
    router_term = dot(logit_high, rows_x(), ROW_DIMS) + dot(logit_low, rows_x(), ROW_DIMS)
    spare = (
        lax.broadcasted_iota(jnp.int32, (rows, count), 0)
        == lax.broadcasted_iota(jnp.int32, (rows, count), 1) * STRIDE + STRIDE - 1
    )
    router_rows = dot(spare.astype(F32).astype(BF16), router_term.astype(BF16))
    row_grads[...] = (
        (total[...] + router_part + router_rows).astype(BF16).reshape(row_grads.shape)
    )


def spread_kernel(back, after, out, packed):
    rows = back.shape[0]
    spare = lax.broadcasted_iota(jnp.int32, (8, rows), 1) % STRIDE == STRIDE - 1
    sums = dot(spare.astype(F32).astype(BF16), back[...])
    lanes = packed.shape[1]
    for c in range(packed.shape[0]):
        packed[c : c + 1, :] = sums[:1, c * lanes : (c + 1) * lanes]
    out[...] = jnp.broadcast_to(packed[...][None], out.shape)


def weight_kernel(parts_of, sources_count, first, *refs):
    units = len(parts_of)
    place, router = refs[:2]
    weights = refs[2:5]
    sources = refs[5 : 5 + sources_count]
    before = None if first else refs[-13]
    out, held, came_x, came_g, even, odd, terms, total, stage, w_sem, r_sem, o_sem = refs[-12:]
    count = router.shape[0]
    hidden = held.shape[1]
    unit = came_x.shape[1] * came_x.shape[2]
    features = came_x.shape[3]
    offset = pl.multiple_of(place[1] * hidden, STRIDE)

    def weight_copy(k):
        return pltpu.make_async_copy(
            weights[k].at[0, pl.ds(offset, hidden), :], held.at[k], w_sem.at[k]
        )

    def row_copy(k, u):
        source, part = parts_of[u]
        size = came_x.shape[1]
        return pltpu.make_async_copy(
            sources[source].at[pl.ds(part * size, size), k],
            (came_x, came_g)[k].at[u],
            r_sem.at[k, u],
        )

    def rows_x(u):
        return came_x[u].reshape(unit, features)

    def rows_g(u):
        return came_g[u].reshape(unit, features)

    def out_copy(k):
        return pltpu.make_async_copy(stage.at[k], out.at[k], o_sem.at[k])

    def before_copy(k):
        return pltpu.make_async_copy(before.at[k], total.at[k], o_sem.at[3 + k])

    row_copy(0, 0).start()
    weight_copy(0).start()
    weight_copy(1).start()
    row_copy(1, 0).start()
    weight_copy(2).start()
    for u in range(1, units):
        row_copy(0, u).start()
        row_copy(1, u).start()
    if not first:
        for k in range(3):
            before_copy(k).start()

    stacked = jnp.concatenate(split_three(router[...]), 0)
    gates = [None] * units

    def prepare(u, slot):
        row_copy(0, u).wait()
        if u == 0:
            weight_copy(0).wait()
        slot[0] = dot(held[0], rows_x(u), FEATURE_DIMS)
        if u == 0:
            weight_copy(1).wait()
        slot[1] = dot(held[1], rows_x(u), FEATURE_DIMS)
        parts = dot(stacked, rows_x(u), FEATURE_DIMS)
        probs = softmax(parts[:count] + parts[count : 2 * count] + parts[2 * count :], 0)
        mine = lax.broadcasted_iota(jnp.int32, probs.shape, 0) == place[0]
        gates[u] = jnp.sum(jnp.where(mine, probs, 0.0), 0, keepdims=True)
        row_copy(1, u).wait()
        if u == 0:
            weight_copy(2).wait()
        slot[2] = dot(held[2], rows_g(u), FEATURE_DIMS)

    def finish(u, slot):
        where = slice(u * unit, (u + 1) * unit)
        gelu_value, gelu_slope = gelu_parts(slot[0])
        up_pre = slot[1]
        hidden_grad = slot[2] * gates[u]
        terms[0, :, where] = (hidden_grad * up_pre * gelu_slope).astype(BF16)
        terms[1, :, where] = (hidden_grad * gelu_value).astype(BF16)
        terms[2, :, where] = (gelu_value * up_pre * gates[u]).astype(BF16)

    slots = (even, odd)
    prepare(0, slots[0])
    for u in range(units):
        if u + 1 < units:
            prepare(u + 1, slots[(u + 1) % 2])
        finish(u, slots[u % 2])
    for k in range(3):
        rows = (came_g if k == 2 else came_x)[...].reshape(units * unit, features)
        value = dot(terms[k], rows)
        if not first:
            before_copy(k).wait()
            value = value + total[k].astype(F32)
        stage[k] = value.astype(stage.dtype)
        out_copy(k).start()
    for k in range(3):
        out_copy(k).wait()


def run_dispatch(tokens, out_grad, routes, experts, capacity):
    shape = jax.ShapeDtypeStruct((experts, 2 * STRIDE, tokens.shape[1]), BF16)
    return pl.pallas_call(
        functools.partial(dispatch_kernel, experts, capacity),
        out_shape=shape,
        compiler_params=pltpu.CompilerParams(vmem_limit_bytes=VMEM_LIMIT),
        name="dispatch",
    )(tokens, out_grad, routes)


def run_combine(routes, back, spread, after, experts, capacity):
    vmem = pl.BlockSpec(memory_space=pltpu.VMEM)
    features = back.shape[1]
    return pl.pallas_call(
        functools.partial(combine_kernel, experts, capacity),
        in_specs=[vmem, vmem, vmem, pl.BlockSpec(memory_space=pl.ANY)],
        out_specs=(vmem, vmem),
        out_shape=(
            jax.ShapeDtypeStruct((routes.shape[1], features), BF16),
            jax.ShapeDtypeStruct((experts, features), F32),
        ),
        compiler_params=pltpu.CompilerParams(vmem_limit_bytes=VMEM_LIMIT),
        name="combine",
    )(routes, back, spread, after)


def run_expert(place, got, router, weights, after=(), tile=256):
    sources, _, stride, features = got.shape
    rows = sources * stride
    hidden = weights[0].shape[1]
    experts = router.shape[0]
    tiles = hidden // tile
    vmem = pl.BlockSpec(memory_space=pltpu.VMEM)
    anywhere = pl.BlockSpec(memory_space=pl.ANY)
    return pl.pallas_call(
        functools.partial(expert_kernel, tile, tiles),
        in_specs=[pl.BlockSpec(memory_space=pltpu.SMEM), vmem]
        + [anywhere] * 3
        + [vmem]
        + [anywhere] * len(after),
        out_specs=vmem,
        out_shape=jax.ShapeDtypeStruct((sources, stride, features), BF16),
        scratch_shapes=[pltpu.VMEM((hidden, features), BF16)] * 3
        + [
            pltpu.VMEM((rows, features), F32),
            pltpu.VMEM((rows, 128), F32),
            pltpu.VMEM((3, rows, tile), F32),
            pltpu.VMEM((3, rows, tile), F32),
            pltpu.SemaphoreType.DMA((3, tiles)),
        ],
        compiler_params=pltpu.CompilerParams(vmem_limit_bytes=VMEM_LIMIT),
        cost_estimate=pl.CostEstimate(
            flops=20 * rows * hidden * features,
            bytes_accessed=6 * hidden * features + 6 * rows * features,
            transcendentals=rows * hidden,
        ),
        name="expert_pass",
    )(place, router, *weights, got, *after)


def pass_kernel(value, after, out):
    pass


def run_after(value, after):
    anywhere = pl.BlockSpec(memory_space=pl.ANY)
    return pl.pallas_call(
        pass_kernel,
        in_specs=[anywhere, anywhere],
        out_specs=anywhere,
        out_shape=jax.ShapeDtypeStruct(value.shape, value.dtype),
        input_output_aliases={0: 0},
        name="after",
    )(value, after)


def run_spread(back, after, devices):
    vmem = pl.BlockSpec(memory_space=pltpu.VMEM)
    return pl.pallas_call(
        spread_kernel,
        in_specs=[vmem, pl.BlockSpec(memory_space=pl.ANY)],
        out_specs=vmem,
        out_shape=jax.ShapeDtypeStruct((devices, 8, back.shape[1] // 8), F32),
        scratch_shapes=[pltpu.VMEM((8, back.shape[1] // 8), F32)],
        compiler_params=pltpu.CompilerParams(vmem_limit_bytes=VMEM_LIMIT),
        name="spread",
    )(back, after)


def run_weight(place, router, weights, pieces, before, slices, after=(), effort=1):
    features = router.shape[1]
    hidden = weights[0].shape[1] // slices
    size, stride = pieces[0].shape[0] // 2, pieces[0].shape[2]
    unit = size * stride
    parts_of = [(i, h) for i, piece in enumerate(pieces) for h in range(piece.shape[0] // size)]
    units = len(parts_of)
    vmem = pl.BlockSpec(memory_space=pltpu.VMEM)
    anywhere = pl.BlockSpec(memory_space=pl.ANY)
    extra = [*after, *([] if before is None else [before])]
    return pl.pallas_call(
        functools.partial(weight_kernel, parts_of, len(pieces), before is None),
        in_specs=[pl.BlockSpec(memory_space=pltpu.SMEM), vmem]
        + [anywhere] * (3 + len(pieces) + len(extra)),
        out_specs=anywhere,
        out_shape=jax.ShapeDtypeStruct((3, hidden, features), BF16),
        scratch_shapes=[
            pltpu.VMEM((3, hidden, features), BF16),
            pltpu.VMEM((units, size, stride, features), BF16),
            pltpu.VMEM((units, size, stride, features), BF16),
            pltpu.VMEM((3, hidden, unit), F32),
            pltpu.VMEM((3, hidden, unit), F32),
            pltpu.VMEM((3, hidden, units * unit), BF16),
            pltpu.VMEM((3, hidden if before is not None else STRIDE, features), BF16),
            pltpu.VMEM((3, hidden, features), BF16),
            pltpu.SemaphoreType.DMA((3,)),
            pltpu.SemaphoreType.DMA((2, units)),
            pltpu.SemaphoreType.DMA((6,)),
        ],
        compiler_params=pltpu.CompilerParams(vmem_limit_bytes=VMEM_LIMIT),
        cost_estimate=pl.CostEstimate(
            flops=effort * units * unit * hidden * features,
            bytes_accessed=units * unit * features,
            transcendentals=0,
        ),
        name="weight_grads",
    )(place, router, *weights, *pieces, *extra)


def shift(value, axis, step):
    size = lax.axis_size(axis)
    return lax.ppermute(value, axis, [(i, (i + step) % size) for i in range(size)])


def share(value, axes):
    return lax.all_to_all(value, axes, split_axis=0, concat_axis=0, tiled=True)


def shards(tokens, out_grad, routes, router_weight, gate_weight, up_weight, down_weight):
    count_tok, features = tokens.shape
    experts = router_weight.shape[1]
    capacity = 5 * count_tok * 2 // (4 * experts)
    routes_t = routes.T
    router = router_weight.T
    weights = (gate_weight, up_weight, down_weight)
    expert = lax.axis_index("expert").astype(jnp.int32)
    group = lax.axis_index("dp").astype(jnp.int32)
    place = jnp.stack([expert, group])
    slices = lax.axis_size("dp")
    devices = slices * lax.axis_size("expert")

    def send(tokens, out_grad, routes):
        sent = run_dispatch(tokens, out_grad, routes, experts, capacity)
        return sent, share(sent, "expert").reshape(experts, 2, STRIDE, features)

    far_inputs = [shift(v, "dp", 2) for v in (tokens, out_grad, routes_t)]
    _, own = send(tokens, out_grad, routes_t)
    far_sent, far = send(*far_inputs)
    left, right = shift(own, "dp", 1), shift(own, "dp", -1)

    row_grads = run_expert(place, own, router, weights, after=(far_sent,))
    row_grads = run_after(row_grads, far)
    back = share(row_grads, "expert").reshape(-1, features)

    weight = functools.partial(run_weight, place, router, weights, slices=slices)
    early = weight([own, far], None, after=(row_grads,), effort=0)
    grads = weight([left, right], early, effort=20)
    spread = share(run_spread(back, early, devices), ("expert", "dp"))
    in_grad, grad_router = run_combine(routes_t, back, spread, grads, experts, capacity)
    return (in_grad, jnp.transpose(grads, (1, 0, 2))[None], grad_router.T)


def solution(mesh):
    in_specs = (
        P(("expert", "dp"), None),
        P(("expert", "dp"), None),
        P(("expert", "dp"), None),
        P(),
        P("expert", None, None),
        P("expert", None, None),
        P("expert", None, None),
    )
    out_specs = (P(("expert", "dp"), None), P("expert", "dp", None, None), P())
    return jax.shard_map(shards, mesh=mesh, in_specs=in_specs, out_specs=out_specs, check_vma=False)
```

```python
import functools
import jax
import jax.numpy as jnp
from jax import lax
from jax.experimental import pallas as pl
from jax.experimental.pallas import tpu as pltpu
from jax.sharding import PartitionSpec as P

SQRT_TWO_OVER_PI = 0.7978845608
CUBIC_COEF = 0.044715
STRIDE = 16
F32 = jnp.float32
BF16 = jnp.bfloat16
VMEM_LIMIT = 60 * 1024 * 1024

FEATURE_DIMS = (((1,), (1,)), ((), ()))
ROW_DIMS = (((0,), (0,)), ((), ()))


def dot(left, right, dims=(((1,), (0,)), ((), ()))):
    return lax.dot_general(left, right, dims, preferred_element_type=F32)


def gelu_parts(values):
    square = values * values
    tanh_value = jnp.tanh(values * (SQRT_TWO_OVER_PI + (SQRT_TWO_OVER_PI * CUBIC_COEF) * square))
    half = 0.5 + 0.5 * tanh_value
    slope = half + (half * (1.0 - tanh_value)) * values * (
        SQRT_TWO_OVER_PI + (3.0 * CUBIC_COEF * SQRT_TWO_OVER_PI) * square
    )
    return (values * half, slope)


def split_three(values):
    high = values.astype(BF16)
    rest = values - high.astype(F32)
    mid = rest.astype(BF16)
    low = (rest - mid.astype(F32)).astype(BF16)
    return (high, mid, low)


def softmax(logits, axis):
    shifted = jnp.exp(logits - jnp.max(logits, axis, keepdims=True))
    return shifted / jnp.sum(shifted, axis, keepdims=True)


def slot_rows(routes, experts, capacity):
    count_tok = routes.shape[1]
    expert_ids = lax.broadcasted_iota(jnp.int32, (experts, count_tok), 0)
    first = expert_ids == routes[0:1, :]
    second = expert_ids == routes[1:2, :]
    earlier = (
        lax.broadcasted_iota(jnp.int32, (count_tok, count_tok), 0)
        < lax.broadcasted_iota(jnp.int32, (count_tok, count_tok), 1)
    ).astype(BF16)
    first_hits = first.astype(F32)
    second_hits = second.astype(F32)
    first_before = dot(first_hits.astype(BF16), earlier)
    second_before = dot(second_hits.astype(BF16), earlier) + jnp.sum(first_hits, 1, keepdims=True)
    first_pos = jnp.sum(first_hits * first_before, 0, keepdims=True)
    second_pos = jnp.sum(second_hits * second_before, 0, keepdims=True)
    slots = []
    for pos, route in ((first_pos, routes[0:1, :]), (second_pos, routes[1:2, :])):
        pos = pos.astype(jnp.int32)
        slots.append(jnp.where(pos < capacity, route * STRIDE + pos, -1))
    return slots


def slot_mask(slots, experts):
    count_tok = slots[0].shape[1]
    slot_ids = lax.broadcasted_iota(jnp.int32, (experts * STRIDE, count_tok), 0)
    return ((slot_ids == slots[0]) | (slot_ids == slots[1])).astype(F32).astype(BF16)


def dispatch_kernel(experts, capacity, tokens, out_grad, routes, sent):
    mask = slot_mask(slot_rows(routes[...], experts, capacity), experts)
    for k, source in enumerate((tokens, out_grad)):
        rows = dot(mask, source[...]).astype(BF16).reshape(experts, STRIDE, source.shape[1])
        sent[:, k * STRIDE : (k + 1) * STRIDE, :] = rows


def combine_kernel(experts, capacity, routes, back, after, in_grad, spread, packed):
    rows = back.shape[0]
    spare = lax.broadcasted_iota(jnp.int32, (8, rows), 1) % STRIDE == STRIDE - 1
    sums = dot(spare.astype(F32).astype(BF16), back[...])
    lanes = packed.shape[1]
    for c in range(packed.shape[0]):
        packed[c : c + 1, :] = sums[:1, c * lanes : (c + 1) * lanes]
    spread[...] = jnp.broadcast_to(packed[...][None], spread.shape)
    mask = slot_mask(slot_rows(routes[...], experts, capacity), experts)
    in_grad[...] = dot(mask, back[...], ROW_DIMS).astype(BF16)


def total_kernel(spread, after, grad_router):
    experts = grad_router.shape[0]
    devices, chunks, lanes = spread.shape
    summed = jnp.sum(spread[...].reshape(experts, devices // experts, chunks, lanes), 1)
    for c in range(chunks):
        grad_router[:, c * lanes : (c + 1) * lanes] = summed[:, c, :]


def expert_kernel(tile, tiles, *refs):
    place, router = refs[:2]
    weights = refs[2:5]
    got = refs[5]
    (
        row_grads,
        w_gate,
        w_up,
        w_down,
        total,
        hits,
        even,
        odd,
        arrived,
    ) = refs[-9:]
    held = (w_gate, w_up, w_down)
    rows = hits.shape[0]
    count = router.shape[0]
    lanes = hits.shape[1]

    features = got.shape[3]

    def rows_x():
        return got[:, 0].reshape(rows, features)

    def rows_g():
        return got[:, 1].reshape(rows, features)

    def weight_copies(i):
        part = pl.ds(i * tile, tile)
        return [
            pltpu.make_async_copy(weights[k].at[0, part, :], held[k].at[part, :], arrived.at[k, i])
            for k in range(3)
        ]

    for i in range(tiles):
        for copy in weight_copies(i):
            copy.start()
    total[...] = jnp.zeros_like(total)
    hits[...] = jnp.zeros_like(hits)
    high, mid, low = split_three(router[...])
    parts = dot(rows_x(), jnp.concatenate([high, mid, low], 0), FEATURE_DIMS)
    probs = softmax(parts[:, :count] + parts[:, count : 2 * count] + parts[:, 2 * count :], 1)
    mine = lax.broadcasted_iota(jnp.int32, probs.shape, 1) == place[0]
    gate = jnp.sum(jnp.where(mine, probs, 0.0), 1, keepdims=True)
    gate_wide = jnp.broadcast_to(gate, (rows, tile))

    def wait(i):
        for copy in weight_copies(i):
            copy.wait()

    def part(i):
        return pl.ds(pl.multiple_of(i * tile, tile), tile)

    def before(i, slot):
        slot[0] = dot(rows_x(), w_gate[part(i), :], FEATURE_DIMS)
        slot[1] = dot(rows_x(), w_up[part(i), :], FEATURE_DIMS)
        slot[2] = dot(rows_g(), w_down[part(i), :], FEATURE_DIMS)

    def after(i, slot):
        gelu_value, gelu_slope = gelu_parts(slot[0])
        up_pre = slot[1]
        raw_grad = slot[2]
        hit = gelu_value * up_pre * raw_grad
        hits[...] += sum(hit[:, c : c + lanes] for c in range(0, tile, lanes))
        hidden_grad = raw_grad * gate_wide
        pre_gate_grad = (hidden_grad * up_pre * gelu_slope).astype(BF16)
        pre_up_grad = (hidden_grad * gelu_value).astype(BF16)
        total[...] += dot(pre_gate_grad, w_gate[part(i), :]) + dot(pre_up_grad, w_up[part(i), :])

    wait(0)
    before(0, even)

    def pair(j, carry):
        wait(2 * j + 1)
        wait(2 * j + 2)
        before(2 * j + 1, odd)
        after(2 * j, even)
        before(2 * j + 2, even)
        after(2 * j + 1, odd)
        return carry

    lax.fori_loop(0, (tiles - 1) // 2, pair, 0)
    if tiles % 2 == 0:
        wait(tiles - 1)
        before(tiles - 1, odd)
        after(tiles - 2, even)
        after(tiles - 1, odd)
    else:
        after(tiles - 1, even)

    logit_grads = jnp.sum(hits[...], 1, keepdims=True) * gate * (mine.astype(F32) - probs)
    logit_high = logit_grads.astype(BF16)
    logit_low = (logit_grads - logit_high.astype(F32)).astype(BF16)
    router_part = dot(logit_high, high) + dot(logit_high, mid) + dot(logit_low, high)
    router_term = dot(logit_high, rows_x(), ROW_DIMS) + dot(logit_low, rows_x(), ROW_DIMS)
    spare = (
        lax.broadcasted_iota(jnp.int32, (rows, count), 0)
        == lax.broadcasted_iota(jnp.int32, (rows, count), 1) * STRIDE + STRIDE - 1
    )
    router_rows = dot(spare.astype(F32).astype(BF16), router_term.astype(BF16))
    row_grads[...] = (
        (total[...] + router_part + router_rows).astype(BF16).reshape(row_grads.shape)
    )


def weight_kernel(parts_of, sources_count, first, *refs):
    units = len(parts_of)
    place, router = refs[:2]
    weights = refs[2:5]
    sources = refs[5 : 5 + sources_count]
    before = None if first else refs[-10]
    out, held, even, odd, terms, total, stage, w_sem, o_sem = refs[-9:]
    count = router.shape[0]
    hidden = held.shape[1]
    unit = even.shape[2]
    features = sources[0].shape[3]
    offset = pl.multiple_of(place[1] * hidden, STRIDE)

    def weight_copy(k):
        return pltpu.make_async_copy(
            weights[k].at[0, pl.ds(offset, hidden), :], held.at[k], w_sem.at[k]
        )

    def rows(k, u):
        source, part = parts_of[u]
        size = sources[source].shape[0] // 2
        return sources[source][part * size : (part + 1) * size, k].reshape(unit, features)

    def rows_x(u):
        return rows(0, u)

    def rows_g(u):
        return rows(1, u)

    def out_copy(k):
        return pltpu.make_async_copy(stage.at[k], out.at[k], o_sem.at[k])

    def before_copy(k):
        return pltpu.make_async_copy(before.at[k], total.at[k], o_sem.at[3 + k])

    for k in range(3):
        weight_copy(k).start()
    stacked = jnp.concatenate(split_three(router[...]), 0)
    gates = [None] * units

    def prepare(u, slot):
        if u == 0:
            weight_copy(0).wait()
        slot[0] = dot(held[0], rows_x(u), FEATURE_DIMS)
        if u == 0:
            weight_copy(1).wait()
        slot[1] = dot(held[1], rows_x(u), FEATURE_DIMS)
        parts = dot(stacked, rows_x(u), FEATURE_DIMS)
        probs = softmax(parts[:count] + parts[count : 2 * count] + parts[2 * count :], 0)
        mine = lax.broadcasted_iota(jnp.int32, probs.shape, 0) == place[0]
        gates[u] = jnp.sum(jnp.where(mine, probs, 0.0), 0, keepdims=True)
        if u == 0:
            weight_copy(2).wait()
        if u == 1 and not first:
            for k in range(3):
                before_copy(k).start()
        slot[2] = dot(held[2], rows_g(u), FEATURE_DIMS)

    def finish(u, slot):
        where = slice(u * unit, (u + 1) * unit)
        gelu_value, gelu_slope = gelu_parts(slot[0])
        up_pre = slot[1]
        hidden_grad = slot[2] * gates[u]
        terms[0, :, where] = (hidden_grad * up_pre * gelu_slope).astype(BF16)
        terms[1, :, where] = (hidden_grad * gelu_value).astype(BF16)
        terms[2, :, where] = (gelu_value * up_pre * gates[u]).astype(BF16)

    slots = (even, odd)
    prepare(0, slots[0])
    for u in range(units):
        if u + 1 < units:
            prepare(u + 1, slots[(u + 1) % 2])
        finish(u, slots[u % 2])
    for k in range(3):
        value = None
        for i, source in enumerate(sources):
            count_rows = 2 * unit
            part = dot(
                terms[k, :, i * count_rows : (i + 1) * count_rows],
                source[:, k // 2].reshape(count_rows, features),
            )
            value = part if value is None else value + part
        if not first:
            before_copy(k).wait()
            value = value + total[k].astype(F32)
        stage[k] = value.astype(stage.dtype)
        out_copy(k).start()
    for k in range(3):
        out_copy(k).wait()


def run_dispatch(tokens, out_grad, routes, experts, capacity):
    shape = jax.ShapeDtypeStruct((experts, 2 * STRIDE, tokens.shape[1]), BF16)
    return pl.pallas_call(
        functools.partial(dispatch_kernel, experts, capacity),
        out_shape=shape,
        compiler_params=pltpu.CompilerParams(vmem_limit_bytes=VMEM_LIMIT),
        name="dispatch",
    )(tokens, out_grad, routes)


def run_combine(routes, back, after, experts, capacity, devices):
    vmem = pl.BlockSpec(memory_space=pltpu.VMEM)
    features = back.shape[1]
    return pl.pallas_call(
        functools.partial(combine_kernel, experts, capacity),
        in_specs=[vmem, vmem, pl.BlockSpec(memory_space=pl.ANY)],
        out_specs=(vmem, vmem),
        out_shape=(
            jax.ShapeDtypeStruct((routes.shape[1], features), BF16),
            jax.ShapeDtypeStruct((devices, 8, features // 8), F32),
        ),
        scratch_shapes=[pltpu.VMEM((8, features // 8), F32)],
        compiler_params=pltpu.CompilerParams(vmem_limit_bytes=VMEM_LIMIT),
        name="combine",
    )(routes, back, after)


def run_total(spread, after, experts):
    vmem = pl.BlockSpec(memory_space=pltpu.VMEM)
    devices, chunks, lanes = spread.shape
    return pl.pallas_call(
        total_kernel,
        in_specs=[vmem, pl.BlockSpec(memory_space=pl.ANY)],
        out_specs=vmem,
        out_shape=jax.ShapeDtypeStruct((experts, chunks * lanes), F32),
        compiler_params=pltpu.CompilerParams(vmem_limit_bytes=VMEM_LIMIT),
        name="total",
    )(spread, after)


def run_expert(place, got, router, weights, after=(), tile=256):
    sources, _, stride, features = got.shape
    rows = sources * stride
    hidden = weights[0].shape[1]
    experts = router.shape[0]
    tiles = hidden // tile
    vmem = pl.BlockSpec(memory_space=pltpu.VMEM)
    anywhere = pl.BlockSpec(memory_space=pl.ANY)
    return pl.pallas_call(
        functools.partial(expert_kernel, tile, tiles),
        in_specs=[pl.BlockSpec(memory_space=pltpu.SMEM), vmem]
        + [anywhere] * 3
        + [vmem]
        + [anywhere] * len(after),
        out_specs=vmem,
        out_shape=jax.ShapeDtypeStruct((sources, stride, features), BF16),
        scratch_shapes=[pltpu.VMEM((hidden, features), BF16)] * 3
        + [
            pltpu.VMEM((rows, features), F32),
            pltpu.VMEM((rows, 128), F32),
            pltpu.VMEM((3, rows, tile), F32),
            pltpu.VMEM((3, rows, tile), F32),
            pltpu.SemaphoreType.DMA((3, tiles)),
        ],
        compiler_params=pltpu.CompilerParams(vmem_limit_bytes=VMEM_LIMIT),
        cost_estimate=pl.CostEstimate(
            flops=20 * rows * hidden * features,
            bytes_accessed=6 * hidden * features + 6 * rows * features,
            transcendentals=rows * hidden,
        ),
        name="expert_pass",
    )(place, router, *weights, got, *after)


def pass_kernel(value, after, out):
    pass


def run_after(value, after):
    anywhere = pl.BlockSpec(memory_space=pl.ANY)
    return pl.pallas_call(
        pass_kernel,
        in_specs=[anywhere, anywhere],
        out_specs=anywhere,
        out_shape=jax.ShapeDtypeStruct(value.shape, value.dtype),
        input_output_aliases={0: 0},
        name="after",
    )(value, after)


def run_weight(place, router, weights, pieces, before, slices, after=(), effort=1):
    features = router.shape[1]
    hidden = weights[0].shape[1] // slices
    size, stride = pieces[0].shape[0] // 2, pieces[0].shape[2]
    unit = size * stride
    parts_of = [(i, h) for i, piece in enumerate(pieces) for h in range(piece.shape[0] // size)]
    units = len(parts_of)
    vmem = pl.BlockSpec(memory_space=pltpu.VMEM)
    anywhere = pl.BlockSpec(memory_space=pl.ANY)
    extra = [*after, *([] if before is None else [before])]
    return pl.pallas_call(
        functools.partial(weight_kernel, parts_of, len(pieces), before is None),
        in_specs=[pl.BlockSpec(memory_space=pltpu.SMEM), vmem]
        + [anywhere] * 3
        + [vmem] * len(pieces)
        + [anywhere] * len(extra),
        out_specs=anywhere,
        out_shape=jax.ShapeDtypeStruct((3, hidden, features), BF16),
        scratch_shapes=[
            pltpu.VMEM((3, hidden, features), BF16),
            pltpu.VMEM((3, hidden, unit), F32),
            pltpu.VMEM((3, hidden, unit), F32),
            pltpu.VMEM((3, hidden, units * unit), BF16),
            pltpu.VMEM((3, hidden if before is not None else STRIDE, features), BF16),
            pltpu.VMEM((3, hidden, features), BF16),
            pltpu.SemaphoreType.DMA((3,)),
            pltpu.SemaphoreType.DMA((6,)),
        ],
        compiler_params=pltpu.CompilerParams(vmem_limit_bytes=VMEM_LIMIT),
        cost_estimate=pl.CostEstimate(
            flops=effort * units * unit * hidden * features,
            bytes_accessed=units * unit * features,
            transcendentals=0,
        ),
        name="weight_grads",
    )(place, router, *weights, *pieces, *extra)


def shift(value, axis, step):
    size = lax.axis_size(axis)
    return lax.ppermute(value, axis, [(i, (i + step) % size) for i in range(size)])


def share(value, axes):
    return lax.all_to_all(value, axes, split_axis=0, concat_axis=0, tiled=True)


def shards(tokens, out_grad, routes, router_weight, gate_weight, up_weight, down_weight):
    count_tok, features = tokens.shape
    experts = router_weight.shape[1]
    capacity = 5 * count_tok * 2 // (4 * experts)
    routes_t = routes.T
    router = router_weight.T
    weights = (gate_weight, up_weight, down_weight)
    expert = lax.axis_index("expert").astype(jnp.int32)
    group = lax.axis_index("dp").astype(jnp.int32)
    place = jnp.stack([expert, group])
    slices = lax.axis_size("dp")
    devices = slices * lax.axis_size("expert")

    def send(tokens, out_grad, routes):
        sent = run_dispatch(tokens, out_grad, routes, experts, capacity)
        return sent, share(sent, "expert").reshape(experts, 2, STRIDE, features)

    far_inputs = [shift(v, "dp", 2) for v in (tokens, out_grad, routes_t)]
    _, own = send(tokens, out_grad, routes_t)
    far_sent, far = send(*far_inputs)
    left, right = shift(own, "dp", 1), shift(own, "dp", -1)

    row_grads = run_expert(place, own, router, weights, after=(far_sent,))
    row_grads = run_after(row_grads, far)
    back = share(row_grads, "expert").reshape(-1, features)

    weight = functools.partial(run_weight, place, router, weights, slices=slices)
    early = weight([own, far], None, after=(row_grads,), effort=0)
    grads = weight([left, right], early, effort=20)
    in_grad, spread = run_combine(routes_t, back, early, experts, capacity, devices)
    grad_router = run_total(share(spread, ("expert", "dp")), grads, experts)
    return (in_grad, jnp.transpose(grads, (1, 0, 2))[None], grad_router.T)


def solution(mesh):
    in_specs = (
        P(("expert", "dp"), None),
        P(("expert", "dp"), None),
        P(("expert", "dp"), None),
        P(),
        P("expert", None, None),
        P("expert", None, None),
        P("expert", None, None),
    )
    out_specs = (P(("expert", "dp"), None), P("expert", "dp", None, None), P())
    return jax.shard_map(shards, mesh=mesh, in_specs=in_specs, out_specs=out_specs, check_vma=False)
```

```python
import functools
import jax
import jax.numpy as jnp
from jax import lax
from jax.experimental import pallas as pl
from jax.experimental.pallas import tpu as pltpu
from jax.sharding import PartitionSpec as P

SQRT_TWO_OVER_PI = 0.7978845608
CUBIC_COEF = 0.044715
STRIDE = 16
F32 = jnp.float32
BF16 = jnp.bfloat16
VMEM_LIMIT = 64 * 1024 * 1024

FEATURE_DIMS = (((1,), (1,)), ((), ()))
ROW_DIMS = (((0,), (0,)), ((), ()))


def dot(left, right, dims=(((1,), (0,)), ((), ()))):
    return lax.dot_general(left, right, dims, preferred_element_type=F32)


def gelu_parts(values):
    square = values * values
    tanh_value = jnp.tanh(values * (SQRT_TWO_OVER_PI + (SQRT_TWO_OVER_PI * CUBIC_COEF) * square))
    half = 0.5 + 0.5 * tanh_value
    slope = half + (half * (1.0 - tanh_value)) * values * (
        SQRT_TWO_OVER_PI + (3.0 * CUBIC_COEF * SQRT_TWO_OVER_PI) * square
    )
    return (values * half, slope)


def split_three(values):
    high = values.astype(BF16)
    rest = values - high.astype(F32)
    mid = rest.astype(BF16)
    low = (rest - mid.astype(F32)).astype(BF16)
    return (high, mid, low)


def softmax(logits, axis):
    shifted = jnp.exp(logits - jnp.max(logits, axis, keepdims=True))
    return shifted / jnp.sum(shifted, axis, keepdims=True)


def slot_rows(routes, experts, capacity):
    count_tok = routes.shape[1]
    expert_ids = lax.broadcasted_iota(jnp.int32, (experts, count_tok), 0)
    first = expert_ids == routes[0:1, :]
    second = expert_ids == routes[1:2, :]
    earlier = (
        lax.broadcasted_iota(jnp.int32, (count_tok, count_tok), 0)
        < lax.broadcasted_iota(jnp.int32, (count_tok, count_tok), 1)
    ).astype(BF16)
    first_hits = first.astype(F32)
    second_hits = second.astype(F32)
    first_before = dot(first_hits.astype(BF16), earlier)
    second_before = dot(second_hits.astype(BF16), earlier) + jnp.sum(first_hits, 1, keepdims=True)
    first_pos = jnp.sum(first_hits * first_before, 0, keepdims=True)
    second_pos = jnp.sum(second_hits * second_before, 0, keepdims=True)
    slots = []
    for pos, route in ((first_pos, routes[0:1, :]), (second_pos, routes[1:2, :])):
        pos = pos.astype(jnp.int32)
        slots.append(jnp.where(pos < capacity, route * STRIDE + pos, -1))
    return slots


def slot_mask(slots, experts):
    count_tok = slots[0].shape[1]
    slot_ids = lax.broadcasted_iota(jnp.int32, (experts * STRIDE, count_tok), 0)
    return ((slot_ids == slots[0]) | (slot_ids == slots[1])).astype(F32).astype(BF16)


def dispatch_kernel(experts, capacity, tokens, out_grad, routes, sent):
    mask = slot_mask(slot_rows(routes[...], experts, capacity), experts)
    for k, source in enumerate((tokens, out_grad)):
        rows = dot(mask, source[...]).astype(BF16).reshape(experts, STRIDE, source.shape[1])
        sent[:, k * STRIDE : (k + 1) * STRIDE, :] = rows


def combine_kernel(experts, capacity, routes, back, after, in_grad, spread, packed):
    rows = back.shape[0]
    spare = lax.broadcasted_iota(jnp.int32, (8, rows), 1) % STRIDE == STRIDE - 1
    sums = dot(spare.astype(F32).astype(BF16), back[...])
    lanes = packed.shape[1]
    for c in range(packed.shape[0]):
        packed[c : c + 1, :] = sums[:1, c * lanes : (c + 1) * lanes]
    spread[...] = jnp.broadcast_to(packed[...][None], spread.shape)
    mask = slot_mask(slot_rows(routes[...], experts, capacity), experts)
    in_grad[...] = dot(mask, back[...], ROW_DIMS).astype(BF16)


def total_kernel(spread, after, grad_router):
    experts = grad_router.shape[0]
    devices, chunks, lanes = spread.shape
    summed = jnp.sum(spread[...].reshape(experts, devices // experts, chunks, lanes), 1)
    for c in range(chunks):
        grad_router[:, c * lanes : (c + 1) * lanes] = summed[:, c, :]


def expert_kernel(tile, tiles, *refs):
    place, router = refs[:2]
    weights = refs[2:5]
    got = refs[5]
    (
        row_grads,
        w_gate,
        w_up,
        w_down,
        total,
        hits,
        even,
        odd,
        arrived,
    ) = refs[-9:]
    held = (w_gate, w_up, w_down)
    rows = hits.shape[0]
    count = router.shape[0]
    lanes = hits.shape[1]

    features = got.shape[3]

    def rows_x():
        return got[:, 0].reshape(rows, features)

    def rows_g():
        return got[:, 1].reshape(rows, features)

    def weight_copies(i):
        part = pl.ds(i * tile, tile)
        return [
            pltpu.make_async_copy(weights[k].at[0, part, :], held[k].at[part, :], arrived.at[k, i])
            for k in range(3)
        ]

    for i in range(tiles):
        for copy in weight_copies(i):
            copy.start()
    total[...] = jnp.zeros_like(total)
    hits[...] = jnp.zeros_like(hits)
    high, mid, low = split_three(router[...])
    parts = dot(rows_x(), jnp.concatenate([high, mid, low], 0), FEATURE_DIMS)
    probs = softmax(parts[:, :count] + parts[:, count : 2 * count] + parts[:, 2 * count :], 1)
    mine = lax.broadcasted_iota(jnp.int32, probs.shape, 1) == place[0]
    gate = jnp.sum(jnp.where(mine, probs, 0.0), 1, keepdims=True)
    gate_wide = jnp.broadcast_to(gate, (rows, tile))

    def wait(i):
        for copy in weight_copies(i):
            copy.wait()

    def part(i):
        return pl.ds(pl.multiple_of(i * tile, tile), tile)

    def before(i, slot):
        slot[0] = dot(rows_x(), w_gate[part(i), :], FEATURE_DIMS)
        slot[1] = dot(rows_x(), w_up[part(i), :], FEATURE_DIMS)
        slot[2] = dot(rows_g(), w_down[part(i), :], FEATURE_DIMS)

    def after(i, slot):
        gelu_value, gelu_slope = gelu_parts(slot[0])
        up_pre = slot[1]
        raw_grad = slot[2]
        hit = gelu_value * up_pre * raw_grad
        hits[...] += sum(hit[:, c : c + lanes] for c in range(0, tile, lanes))
        hidden_grad = raw_grad * gate_wide
        pre_gate_grad = (hidden_grad * up_pre * gelu_slope).astype(BF16)
        pre_up_grad = (hidden_grad * gelu_value).astype(BF16)
        total[...] += dot(pre_gate_grad, w_gate[part(i), :]) + dot(pre_up_grad, w_up[part(i), :])

    wait(0)
    before(0, even)

    def pair(j, carry):
        wait(2 * j + 1)
        wait(2 * j + 2)
        before(2 * j + 1, odd)
        after(2 * j, even)
        before(2 * j + 2, even)
        after(2 * j + 1, odd)
        return carry

    lax.fori_loop(0, (tiles - 1) // 2, pair, 0)
    if tiles % 2 == 0:
        wait(tiles - 1)
        before(tiles - 1, odd)
        after(tiles - 2, even)
        after(tiles - 1, odd)
    else:
        after(tiles - 1, even)

    logit_grads = jnp.sum(hits[...], 1, keepdims=True) * gate * (mine.astype(F32) - probs)
    logit_high = logit_grads.astype(BF16)
    logit_low = (logit_grads - logit_high.astype(F32)).astype(BF16)
    router_part = dot(logit_high, high) + dot(logit_high, mid) + dot(logit_low, high)
    router_term = dot(logit_high, rows_x(), ROW_DIMS) + dot(logit_low, rows_x(), ROW_DIMS)
    spare = (
        lax.broadcasted_iota(jnp.int32, (rows, count), 0)
        == lax.broadcasted_iota(jnp.int32, (rows, count), 1) * STRIDE + STRIDE - 1
    )
    router_rows = dot(spare.astype(F32).astype(BF16), router_term.astype(BF16))
    row_grads[...] = (
        (total[...] + router_part + router_rows).astype(BF16).reshape(row_grads.shape)
    )


def weight_kernel(parts_of, sources_count, first, *refs):
    units = len(parts_of)
    place, router = refs[:2]
    weights = refs[2:5]
    sources = refs[5 : 5 + sources_count]
    before = None if first else refs[-10]
    out, held, even, odd, terms, total, stage, w_sem, o_sem = refs[-9:]
    count = router.shape[0]
    hidden = held.shape[1]
    unit = even.shape[2]
    features = sources[0].shape[3]
    offset = pl.multiple_of(place[1] * hidden, STRIDE)

    def weight_copy(k):
        return pltpu.make_async_copy(
            weights[k].at[0, pl.ds(offset, hidden), :], held.at[k], w_sem.at[k]
        )

    def rows(k, u):
        source, part = parts_of[u]
        size = sources[source].shape[0] // 2
        return sources[source][part * size : (part + 1) * size, k].reshape(unit, features)

    def rows_x(u):
        return rows(0, u)

    def rows_g(u):
        return rows(1, u)

    def out_copy(k):
        return pltpu.make_async_copy(stage.at[k], out.at[k], o_sem.at[k])

    def before_copy(k):
        return pltpu.make_async_copy(before.at[k], total.at[k], o_sem.at[3 + k])

    for k in range(3):
        weight_copy(k).start()
    stacked = jnp.concatenate(split_three(router[...]), 0)
    gates = [None] * units

    def prepare(u, slot):
        if u == 0:
            weight_copy(0).wait()
        slot[0] = dot(held[0], rows_x(u), FEATURE_DIMS)
        if u == 0:
            weight_copy(1).wait()
        slot[1] = dot(held[1], rows_x(u), FEATURE_DIMS)
        parts = dot(stacked, rows_x(u), FEATURE_DIMS)
        probs = softmax(parts[:count] + parts[count : 2 * count] + parts[2 * count :], 0)
        mine = lax.broadcasted_iota(jnp.int32, probs.shape, 0) == place[0]
        gates[u] = jnp.sum(jnp.where(mine, probs, 0.0), 0, keepdims=True)
        if u == 0:
            weight_copy(2).wait()
        if u == 1 and not first:
            for k in range(3):
                before_copy(k).start()
        slot[2] = dot(held[2], rows_g(u), FEATURE_DIMS)

    def finish(u, slot):
        where = slice(u * unit, (u + 1) * unit)
        gelu_value, gelu_slope = gelu_parts(slot[0])
        up_pre = slot[1]
        hidden_grad = slot[2] * gates[u]
        terms[0, :, where] = (hidden_grad * up_pre * gelu_slope).astype(BF16)
        terms[1, :, where] = (hidden_grad * gelu_value).astype(BF16)
        terms[2, :, where] = (gelu_value * up_pre * gates[u]).astype(BF16)

    slots = (even, odd)
    prepare(0, slots[0])
    for u in range(units):
        if u + 1 < units:
            prepare(u + 1, slots[(u + 1) % 2])
        finish(u, slots[u % 2])
    if not first:
        for k in range(3):
            before_copy(k).wait()
    for k in range(3):
        value = None
        for i, source in enumerate(sources):
            count_rows = 2 * unit
            part = dot(
                terms[k, :, i * count_rows : (i + 1) * count_rows],
                source[:, k // 2].reshape(count_rows, features),
            )
            value = part if value is None else value + part
        if not first:
            value = value + total[k].astype(F32)
        stage[k] = value.astype(stage.dtype)
        out_copy(k).start()
    for k in range(3):
        out_copy(k).wait()


def run_dispatch(tokens, out_grad, routes, experts, capacity):
    shape = jax.ShapeDtypeStruct((experts, 2 * STRIDE, tokens.shape[1]), BF16)
    return pl.pallas_call(
        functools.partial(dispatch_kernel, experts, capacity),
        out_shape=shape,
        compiler_params=pltpu.CompilerParams(vmem_limit_bytes=VMEM_LIMIT),
        name="dispatch",
    )(tokens, out_grad, routes)


def run_combine(routes, back, after, experts, capacity, devices):
    vmem = pl.BlockSpec(memory_space=pltpu.VMEM)
    features = back.shape[1]
    return pl.pallas_call(
        functools.partial(combine_kernel, experts, capacity),
        in_specs=[vmem, vmem, pl.BlockSpec(memory_space=pl.ANY)],
        out_specs=(vmem, vmem),
        out_shape=(
            jax.ShapeDtypeStruct((routes.shape[1], features), BF16),
            jax.ShapeDtypeStruct((devices, 8, features // 8), F32),
        ),
        scratch_shapes=[pltpu.VMEM((8, features // 8), F32)],
        compiler_params=pltpu.CompilerParams(vmem_limit_bytes=VMEM_LIMIT),
        name="combine",
    )(routes, back, after)


def run_total(spread, after, experts):
    vmem = pl.BlockSpec(memory_space=pltpu.VMEM)
    devices, chunks, lanes = spread.shape
    return pl.pallas_call(
        total_kernel,
        in_specs=[vmem, pl.BlockSpec(memory_space=pl.ANY)],
        out_specs=vmem,
        out_shape=jax.ShapeDtypeStruct((experts, chunks * lanes), F32),
        compiler_params=pltpu.CompilerParams(vmem_limit_bytes=VMEM_LIMIT),
        name="total",
    )(spread, after)


def run_expert(place, got, router, weights, after=(), tile=256):
    sources, _, stride, features = got.shape
    rows = sources * stride
    hidden = weights[0].shape[1]
    experts = router.shape[0]
    tiles = hidden // tile
    vmem = pl.BlockSpec(memory_space=pltpu.VMEM)
    anywhere = pl.BlockSpec(memory_space=pl.ANY)
    return pl.pallas_call(
        functools.partial(expert_kernel, tile, tiles),
        in_specs=[pl.BlockSpec(memory_space=pltpu.SMEM), vmem]
        + [anywhere] * 3
        + [vmem]
        + [anywhere] * len(after),
        out_specs=vmem,
        out_shape=jax.ShapeDtypeStruct((sources, stride, features), BF16),
        scratch_shapes=[pltpu.VMEM((hidden, features), BF16)] * 3
        + [
            pltpu.VMEM((rows, features), F32),
            pltpu.VMEM((rows, 128), F32),
            pltpu.VMEM((3, rows, tile), F32),
            pltpu.VMEM((3, rows, tile), F32),
            pltpu.SemaphoreType.DMA((3, tiles)),
        ],
        compiler_params=pltpu.CompilerParams(vmem_limit_bytes=VMEM_LIMIT),
        cost_estimate=pl.CostEstimate(
            flops=20 * rows * hidden * features,
            bytes_accessed=6 * hidden * features + 6 * rows * features,
            transcendentals=rows * hidden,
        ),
        name="expert_pass",
    )(place, router, *weights, got, *after)


def pass_kernel(value, after, out):
    pass


def run_after(value, after):
    anywhere = pl.BlockSpec(memory_space=pl.ANY)
    return pl.pallas_call(
        pass_kernel,
        in_specs=[anywhere, anywhere],
        out_specs=anywhere,
        out_shape=jax.ShapeDtypeStruct(value.shape, value.dtype),
        input_output_aliases={0: 0},
        name="after",
    )(value, after)


def run_weight(place, router, weights, pieces, before, slices, after=(), effort=1):
    features = router.shape[1]
    hidden = weights[0].shape[1] // slices
    size, stride = pieces[0].shape[0] // 2, pieces[0].shape[2]
    unit = size * stride
    parts_of = [(i, h) for i, piece in enumerate(pieces) for h in range(piece.shape[0] // size)]
    units = len(parts_of)
    vmem = pl.BlockSpec(memory_space=pltpu.VMEM)
    anywhere = pl.BlockSpec(memory_space=pl.ANY)
    extra = [*after, *([] if before is None else [before])]
    return pl.pallas_call(
        functools.partial(weight_kernel, parts_of, len(pieces), before is None),
        in_specs=[pl.BlockSpec(memory_space=pltpu.SMEM), vmem]
        + [anywhere] * 3
        + [vmem] * len(pieces)
        + [anywhere] * len(extra),
        out_specs=anywhere,
        out_shape=jax.ShapeDtypeStruct((3, hidden, features), BF16),
        scratch_shapes=[
            pltpu.VMEM((3, hidden, features), BF16),
            pltpu.VMEM((3, hidden, unit), F32),
            pltpu.VMEM((3, hidden, unit), F32),
            pltpu.VMEM((3, hidden, units * unit), BF16),
            pltpu.VMEM((3, hidden if before is not None else STRIDE, features), BF16),
            pltpu.VMEM((3, hidden, features), BF16),
            pltpu.SemaphoreType.DMA((3,)),
            pltpu.SemaphoreType.DMA((6,)),
        ],
        compiler_params=pltpu.CompilerParams(vmem_limit_bytes=VMEM_LIMIT),
        cost_estimate=pl.CostEstimate(
            flops=effort * units * unit * hidden * features,
            bytes_accessed=units * unit * features,
            transcendentals=0,
        ),
        name="weight_grads",
    )(place, router, *weights, *pieces, *extra)


def shift(value, axis, step):
    size = lax.axis_size(axis)
    return lax.ppermute(value, axis, [(i, (i + step) % size) for i in range(size)])


def share(value, axes):
    return lax.all_to_all(value, axes, split_axis=0, concat_axis=0, tiled=True)


def shards(tokens, out_grad, routes, router_weight, gate_weight, up_weight, down_weight):
    count_tok, features = tokens.shape
    experts = router_weight.shape[1]
    capacity = 5 * count_tok * 2 // (4 * experts)
    routes_t = routes.T
    router = router_weight.T
    weights = (gate_weight, up_weight, down_weight)
    expert = lax.axis_index("expert").astype(jnp.int32)
    group = lax.axis_index("dp").astype(jnp.int32)
    place = jnp.stack([expert, group])
    slices = lax.axis_size("dp")
    devices = slices * lax.axis_size("expert")

    def send(tokens, out_grad, routes):
        sent = run_dispatch(tokens, out_grad, routes, experts, capacity)
        return sent, share(sent, "expert").reshape(experts, 2, STRIDE, features)

    far_inputs = [shift(v, "dp", 2) for v in (tokens, out_grad, routes_t)]
    _, own = send(tokens, out_grad, routes_t)
    far_sent, far = send(*far_inputs)
    left, right = shift(own, "dp", 1), shift(own, "dp", -1)

    row_grads = run_expert(place, own, router, weights, after=(far_sent,))
    row_grads = run_after(row_grads, far)
    back = share(row_grads, "expert").reshape(-1, features)

    weight = functools.partial(run_weight, place, router, weights, slices=slices)
    early = weight([own, far], None, after=(row_grads,), effort=0)
    grads = weight([left, right], early, effort=20)
    in_grad, spread = run_combine(routes_t, back, early, experts, capacity, devices)
    grad_router = run_total(share(spread, ("expert", "dp")), grads, experts)
    return (in_grad, jnp.transpose(grads, (1, 0, 2))[None], grad_router.T)


def solution(mesh):
    in_specs = (
        P(("expert", "dp"), None),
        P(("expert", "dp"), None),
        P(("expert", "dp"), None),
        P(),
        P("expert", None, None),
        P("expert", None, None),
        P("expert", None, None),
    )
    out_specs = (P(("expert", "dp"), None), P("expert", "dp", None, None), P())
    return jax.shard_map(shards, mesh=mesh, in_specs=in_specs, out_specs=out_specs, check_vma=False)
```

```python
import functools
import jax
import jax.numpy as jnp
from jax import lax
from jax.experimental import pallas as pl
from jax.experimental.pallas import tpu as pltpu
from jax.sharding import PartitionSpec as P

SQRT_TWO_OVER_PI = 0.7978845608
CUBIC_COEF = 0.044715
STRIDE = 16
F32 = jnp.float32
BF16 = jnp.bfloat16
VMEM_LIMIT = 64 * 1024 * 1024

FEATURE_DIMS = (((1,), (1,)), ((), ()))
ROW_DIMS = (((0,), (0,)), ((), ()))


def dot(left, right, dims=(((1,), (0,)), ((), ()))):
    return lax.dot_general(left, right, dims, preferred_element_type=F32)


def gelu_parts(values):
    square = values * values
    tanh_value = jnp.tanh(values * (SQRT_TWO_OVER_PI + (SQRT_TWO_OVER_PI * CUBIC_COEF) * square))
    half = 0.5 + 0.5 * tanh_value
    slope = half + (half * (1.0 - tanh_value)) * values * (
        SQRT_TWO_OVER_PI + (3.0 * CUBIC_COEF * SQRT_TWO_OVER_PI) * square
    )
    return (values * half, slope)


def split_three(values):
    high = values.astype(BF16)
    rest = values - high.astype(F32)
    mid = rest.astype(BF16)
    low = (rest - mid.astype(F32)).astype(BF16)
    return (high, mid, low)


def softmax(logits, axis):
    shifted = jnp.exp(logits - jnp.max(logits, axis, keepdims=True))
    return shifted / jnp.sum(shifted, axis, keepdims=True)


def slot_rows(routes, experts, capacity):
    count_tok = routes.shape[1]
    expert_ids = lax.broadcasted_iota(jnp.int32, (experts, count_tok), 0)
    first = expert_ids == routes[0:1, :]
    second = expert_ids == routes[1:2, :]
    earlier = (
        lax.broadcasted_iota(jnp.int32, (count_tok, count_tok), 0)
        < lax.broadcasted_iota(jnp.int32, (count_tok, count_tok), 1)
    ).astype(BF16)
    first_hits = first.astype(F32)
    second_hits = second.astype(F32)
    first_before = dot(first_hits.astype(BF16), earlier)
    second_before = dot(second_hits.astype(BF16), earlier) + jnp.sum(first_hits, 1, keepdims=True)
    first_pos = jnp.sum(first_hits * first_before, 0, keepdims=True)
    second_pos = jnp.sum(second_hits * second_before, 0, keepdims=True)
    slots = []
    for pos, route in ((first_pos, routes[0:1, :]), (second_pos, routes[1:2, :])):
        pos = pos.astype(jnp.int32)
        slots.append(jnp.where(pos < capacity, route * STRIDE + pos, -1))
    return slots


def slot_mask(slots, experts):
    count_tok = slots[0].shape[1]
    slot_ids = lax.broadcasted_iota(jnp.int32, (experts * STRIDE, count_tok), 0)
    return ((slot_ids == slots[0]) | (slot_ids == slots[1])).astype(F32).astype(BF16)


def dispatch_kernel(experts, capacity, tokens, out_grad, routes, sent):
    mask = slot_mask(slot_rows(routes[...], experts, capacity), experts)
    for k, source in enumerate((tokens, out_grad)):
        rows = dot(mask, source[...]).astype(BF16).reshape(experts, STRIDE, source.shape[1])
        sent[:, k * STRIDE : (k + 1) * STRIDE, :] = rows


def combine_kernel(experts, capacity, routes, back, after, in_grad, spread, packed):
    rows = back.shape[0]
    spare = lax.broadcasted_iota(jnp.int32, (8, rows), 1) % STRIDE == STRIDE - 1
    sums = dot(spare.astype(F32).astype(BF16), back[...])
    lanes = packed.shape[1]
    for c in range(packed.shape[0]):
        packed[c : c + 1, :] = sums[:1, c * lanes : (c + 1) * lanes]
    spread[...] = jnp.broadcast_to(packed[...][None], spread.shape)
    mask = slot_mask(slot_rows(routes[...], experts, capacity), experts)
    in_grad[...] = dot(mask, back[...], ROW_DIMS).astype(BF16)


def total_kernel(spread, after, grad_router):
    experts = grad_router.shape[0]
    devices, chunks, lanes = spread.shape
    summed = jnp.sum(spread[...].reshape(experts, devices // experts, chunks, lanes), 1)
    for c in range(chunks):
        grad_router[:, c * lanes : (c + 1) * lanes] = summed[:, c, :]


def expert_kernel(tile, tiles, *refs):
    place, router = refs[:2]
    weights = refs[2:5]
    got = refs[5]
    (
        row_grads,
        w_gate,
        w_up,
        w_down,
        total,
        hits,
        even,
        odd,
        arrived,
    ) = refs[-9:]
    held = (w_gate, w_up, w_down)
    rows = hits.shape[0]
    count = router.shape[0]
    lanes = hits.shape[1]

    features = got.shape[3]

    def rows_x():
        return got[:, 0].reshape(rows, features)

    def rows_g():
        return got[:, 1].reshape(rows, features)

    def weight_copies(i):
        part = pl.ds(i * tile, tile)
        return [
            pltpu.make_async_copy(weights[k].at[0, part, :], held[k].at[part, :], arrived.at[k, i])
            for k in range(3)
        ]

    for i in range(tiles):
        for copy in weight_copies(i):
            copy.start()
    total[...] = jnp.zeros_like(total)
    hits[...] = jnp.zeros_like(hits)
    high, mid, low = split_three(router[...])
    parts = dot(rows_x(), jnp.concatenate([high, mid, low], 0), FEATURE_DIMS)
    probs = softmax(parts[:, :count] + parts[:, count : 2 * count] + parts[:, 2 * count :], 1)
    mine = lax.broadcasted_iota(jnp.int32, probs.shape, 1) == place[0]
    gate = jnp.sum(jnp.where(mine, probs, 0.0), 1, keepdims=True)
    gate_wide = jnp.broadcast_to(gate, (rows, tile))

    def wait(i):
        for copy in weight_copies(i):
            copy.wait()

    def part(i):
        return pl.ds(pl.multiple_of(i * tile, tile), tile)

    def before(i, slot):
        slot[0] = dot(rows_x(), w_gate[part(i), :], FEATURE_DIMS)
        slot[1] = dot(rows_x(), w_up[part(i), :], FEATURE_DIMS)
        slot[2] = dot(rows_g(), w_down[part(i), :], FEATURE_DIMS)

    def after(i, slot):
        gelu_value, gelu_slope = gelu_parts(slot[0])
        up_pre = slot[1]
        raw_grad = slot[2]
        hit = gelu_value * up_pre * raw_grad
        hits[...] += sum(hit[:, c : c + lanes] for c in range(0, tile, lanes))
        hidden_grad = raw_grad * gate_wide
        pre_gate_grad = (hidden_grad * up_pre * gelu_slope).astype(BF16)
        pre_up_grad = (hidden_grad * gelu_value).astype(BF16)
        total[...] += dot(pre_gate_grad, w_gate[part(i), :]) + dot(pre_up_grad, w_up[part(i), :])

    wait(0)
    before(0, even)

    def pair(j, carry):
        wait(2 * j + 1)
        wait(2 * j + 2)
        before(2 * j + 1, odd)
        after(2 * j, even)
        before(2 * j + 2, even)
        after(2 * j + 1, odd)
        return carry

    lax.fori_loop(0, (tiles - 1) // 2, pair, 0)
    if tiles % 2 == 0:
        wait(tiles - 1)
        before(tiles - 1, odd)
        after(tiles - 2, even)
        after(tiles - 1, odd)
    else:
        after(tiles - 1, even)

    logit_grads = jnp.sum(hits[...], 1, keepdims=True) * gate * (mine.astype(F32) - probs)
    logit_high = logit_grads.astype(BF16)
    logit_low = (logit_grads - logit_high.astype(F32)).astype(BF16)
    router_part = dot(logit_high, high) + dot(logit_high, mid) + dot(logit_low, high)
    router_term = dot(logit_high, rows_x(), ROW_DIMS) + dot(logit_low, rows_x(), ROW_DIMS)
    spare = (
        lax.broadcasted_iota(jnp.int32, (rows, count), 0)
        == lax.broadcasted_iota(jnp.int32, (rows, count), 1) * STRIDE + STRIDE - 1
    )
    router_rows = dot(spare.astype(F32).astype(BF16), router_term.astype(BF16))
    row_grads[...] = (
        (total[...] + router_part + router_rows).astype(BF16).reshape(row_grads.shape)
    )


def weight_kernel(parts_of, sources_count, first, *refs):
    units = len(parts_of)
    place, router = refs[:2]
    weights = refs[2:5]
    sources = refs[5 : 5 + sources_count]
    before = None if first else refs[-10]
    out, held, even, odd, terms, total, stage, w_sem, o_sem = refs[-9:]
    count = router.shape[0]
    hidden = held.shape[1]
    unit = even.shape[2]
    features = sources[0].shape[3]
    offset = pl.multiple_of(place[1] * hidden, STRIDE)

    def weight_copy(k):
        return pltpu.make_async_copy(
            weights[k].at[0, pl.ds(offset, hidden), :], held.at[k], w_sem.at[k]
        )

    def rows(k, u):
        source, part = parts_of[u]
        size = sources[source].shape[0]
        return sources[source][part * size : (part + 1) * size, k].reshape(unit, features)

    def rows_x(u):
        return rows(0, u)

    def rows_g(u):
        return rows(1, u)

    def out_copy(k):
        return pltpu.make_async_copy(stage.at[k], out.at[k], o_sem.at[k])

    def before_copy(k):
        return pltpu.make_async_copy(before.at[k], total.at[k], o_sem.at[3 + k])

    for k in range(3):
        weight_copy(k).start()
    stacked = jnp.concatenate(split_three(router[...]), 0)
    gates = [None] * units

    def prepare(u, slot):
        if u == 0:
            weight_copy(0).wait()
        slot[0] = dot(held[0], rows_x(u), FEATURE_DIMS)
        if u == 0:
            weight_copy(1).wait()
        slot[1] = dot(held[1], rows_x(u), FEATURE_DIMS)
        parts = dot(stacked, rows_x(u), FEATURE_DIMS)
        probs = softmax(parts[:count] + parts[count : 2 * count] + parts[2 * count :], 0)
        mine = lax.broadcasted_iota(jnp.int32, probs.shape, 0) == place[0]
        gates[u] = jnp.sum(jnp.where(mine, probs, 0.0), 0, keepdims=True)
        if u == 0:
            weight_copy(2).wait()
        if u == 1 and not first:
            for k in range(3):
                before_copy(k).start()
        slot[2] = dot(held[2], rows_g(u), FEATURE_DIMS)

    def finish(u, slot):
        where = slice(u * unit, (u + 1) * unit)
        gelu_value, gelu_slope = gelu_parts(slot[0])
        up_pre = slot[1]
        hidden_grad = slot[2] * gates[u]
        terms[0, :, where] = (hidden_grad * up_pre * gelu_slope).astype(BF16)
        terms[1, :, where] = (hidden_grad * gelu_value).astype(BF16)
        terms[2, :, where] = (gelu_value * up_pre * gates[u]).astype(BF16)

    slots = (even, odd)
    prepare(0, slots[0])
    for u in range(units):
        if u + 1 < units:
            prepare(u + 1, slots[(u + 1) % 2])
        finish(u, slots[u % 2])
    if not first:
        for k in range(3):
            before_copy(k).wait()
    for k in range(3):
        value = None
        for i, source in enumerate(sources):
            count_rows = unit
            part = dot(
                terms[k, :, i * count_rows : (i + 1) * count_rows],
                source[:, k // 2].reshape(count_rows, features),
            )
            value = part if value is None else value + part
        if not first:
            value = value + total[k].astype(F32)
        stage[k] = value.astype(stage.dtype)
        out_copy(k).start()
    for k in range(3):
        out_copy(k).wait()


def run_dispatch(tokens, out_grad, routes, experts, capacity):
    shape = jax.ShapeDtypeStruct((experts, 2 * STRIDE, tokens.shape[1]), BF16)
    return pl.pallas_call(
        functools.partial(dispatch_kernel, experts, capacity),
        out_shape=shape,
        compiler_params=pltpu.CompilerParams(vmem_limit_bytes=VMEM_LIMIT),
        name="dispatch",
    )(tokens, out_grad, routes)


def run_combine(routes, back, after, experts, capacity, devices):
    vmem = pl.BlockSpec(memory_space=pltpu.VMEM)
    features = back.shape[1]
    return pl.pallas_call(
        functools.partial(combine_kernel, experts, capacity),
        in_specs=[vmem, vmem, pl.BlockSpec(memory_space=pl.ANY)],
        out_specs=(vmem, vmem),
        out_shape=(
            jax.ShapeDtypeStruct((routes.shape[1], features), BF16),
            jax.ShapeDtypeStruct((devices, 8, features // 8), F32),
        ),
        scratch_shapes=[pltpu.VMEM((8, features // 8), F32)],
        compiler_params=pltpu.CompilerParams(vmem_limit_bytes=VMEM_LIMIT),
        name="combine",
    )(routes, back, after)


def run_total(spread, after, experts):
    vmem = pl.BlockSpec(memory_space=pltpu.VMEM)
    devices, chunks, lanes = spread.shape
    return pl.pallas_call(
        total_kernel,
        in_specs=[vmem, pl.BlockSpec(memory_space=pl.ANY)],
        out_specs=vmem,
        out_shape=jax.ShapeDtypeStruct((experts, chunks * lanes), F32),
        compiler_params=pltpu.CompilerParams(vmem_limit_bytes=VMEM_LIMIT),
        name="total",
    )(spread, after)


def run_expert(place, got, router, weights, after=(), tile=256):
    sources, _, stride, features = got.shape
    rows = sources * stride
    hidden = weights[0].shape[1]
    experts = router.shape[0]
    tiles = hidden // tile
    vmem = pl.BlockSpec(memory_space=pltpu.VMEM)
    anywhere = pl.BlockSpec(memory_space=pl.ANY)
    return pl.pallas_call(
        functools.partial(expert_kernel, tile, tiles),
        in_specs=[pl.BlockSpec(memory_space=pltpu.SMEM), vmem]
        + [anywhere] * 3
        + [vmem]
        + [anywhere] * len(after),
        out_specs=vmem,
        out_shape=jax.ShapeDtypeStruct((sources, stride, features), BF16),
        scratch_shapes=[pltpu.VMEM((hidden, features), BF16)] * 3
        + [
            pltpu.VMEM((rows, features), F32),
            pltpu.VMEM((rows, 128), F32),
            pltpu.VMEM((3, rows, tile), F32),
            pltpu.VMEM((3, rows, tile), F32),
            pltpu.SemaphoreType.DMA((3, tiles)),
        ],
        compiler_params=pltpu.CompilerParams(vmem_limit_bytes=VMEM_LIMIT),
        cost_estimate=pl.CostEstimate(
            flops=20 * rows * hidden * features,
            bytes_accessed=6 * hidden * features + 6 * rows * features,
            transcendentals=rows * hidden,
        ),
        name="expert_pass",
    )(place, router, *weights, got, *after)


def pass_kernel(value, after, out):
    pass


def run_after(value, after):
    anywhere = pl.BlockSpec(memory_space=pl.ANY)
    return pl.pallas_call(
        pass_kernel,
        in_specs=[anywhere, anywhere],
        out_specs=anywhere,
        out_shape=jax.ShapeDtypeStruct(value.shape, value.dtype),
        input_output_aliases={0: 0},
        name="after",
    )(value, after)


def run_weight(place, router, weights, pieces, before, slices, after=(), effort=1):
    features = router.shape[1]
    hidden = weights[0].shape[1] // slices
    size, stride = pieces[0].shape[0], pieces[0].shape[2]
    unit = size * stride
    parts_of = [(i, h) for i, piece in enumerate(pieces) for h in range(piece.shape[0] // size)]
    units = len(parts_of)
    vmem = pl.BlockSpec(memory_space=pltpu.VMEM)
    anywhere = pl.BlockSpec(memory_space=pl.ANY)
    extra = [*after, *([] if before is None else [before])]
    return pl.pallas_call(
        functools.partial(weight_kernel, parts_of, len(pieces), before is None),
        in_specs=[pl.BlockSpec(memory_space=pltpu.SMEM), vmem]
        + [anywhere] * 3
        + [vmem] * len(pieces)
        + [anywhere] * len(extra),
        out_specs=anywhere,
        out_shape=jax.ShapeDtypeStruct((3, hidden, features), BF16),
        scratch_shapes=[
            pltpu.VMEM((3, hidden, features), BF16),
            pltpu.VMEM((3, hidden, unit), F32),
            pltpu.VMEM((3, hidden, unit), F32),
            pltpu.VMEM((3, hidden, units * unit), BF16),
            pltpu.VMEM((3, hidden if before is not None else STRIDE, features), BF16),
            pltpu.VMEM((3, hidden, features), BF16),
            pltpu.SemaphoreType.DMA((3,)),
            pltpu.SemaphoreType.DMA((6,)),
        ],
        compiler_params=pltpu.CompilerParams(vmem_limit_bytes=VMEM_LIMIT),
        cost_estimate=pl.CostEstimate(
            flops=effort * units * unit * hidden * features,
            bytes_accessed=units * unit * features,
            transcendentals=0,
        ),
        name="weight_grads",
    )(place, router, *weights, *pieces, *extra)


def shift(value, axis, step):
    size = lax.axis_size(axis)
    return lax.ppermute(value, axis, [(i, (i + step) % size) for i in range(size)])


def share(value, axes):
    return lax.all_to_all(value, axes, split_axis=0, concat_axis=0, tiled=True)


def shards(tokens, out_grad, routes, router_weight, gate_weight, up_weight, down_weight):
    count_tok, features = tokens.shape
    experts = router_weight.shape[1]
    capacity = 5 * count_tok * 2 // (4 * experts)
    routes_t = routes.T
    router = router_weight.T
    weights = (gate_weight, up_weight, down_weight)
    expert = lax.axis_index("expert").astype(jnp.int32)
    group = lax.axis_index("dp").astype(jnp.int32)
    place = jnp.stack([expert, group])
    slices = lax.axis_size("dp")
    devices = slices * lax.axis_size("expert")

    def send(tokens, out_grad, routes):
        sent = run_dispatch(tokens, out_grad, routes, experts, capacity)
        return sent, share(sent, "expert").reshape(experts, 2, STRIDE, features)

    far_inputs = [shift(v, "dp", 2) for v in (tokens, out_grad, routes_t)]
    _, own = send(tokens, out_grad, routes_t)
    far_sent, far = send(*far_inputs)
    left, right = shift(own, "dp", 1), shift(own, "dp", -1)

    row_grads = run_expert(place, own, router, weights, after=(far_sent,))
    row_grads = run_after(row_grads, far)
    back = share(row_grads, "expert").reshape(-1, features)

    weight = functools.partial(run_weight, place, router, weights, slices=slices)
    early = weight([own, far], None, after=(row_grads,), effort=0)
    grads = weight([left, right], early, effort=20)
    in_grad, spread = run_combine(routes_t, back, early, experts, capacity, devices)
    grad_router = run_total(share(spread, ("expert", "dp")), grads, experts)
    return (in_grad, jnp.transpose(grads, (1, 0, 2))[None], grad_router.T)


def solution(mesh):
    in_specs = (
        P(("expert", "dp"), None),
        P(("expert", "dp"), None),
        P(("expert", "dp"), None),
        P(),
        P("expert", None, None),
        P("expert", None, None),
        P("expert", None, None),
    )
    out_specs = (P(("expert", "dp"), None), P("expert", "dp", None, None), P())
    return jax.shard_map(shards, mesh=mesh, in_specs=in_specs, out_specs=out_specs, check_vma=False)
```
